128 devices in a mesh: dev: 128 (over y, z, x, core).
Axes of the slice: x: 4, y: 4, z: 4, core: 2. Of those that a mesh axis runs over, the one named last changes fastest.
Arguments:
- spectrum: float32 [32768, 1296], P('dev'), may hold values from 0.01 to 2
- wind_speed: float32 [32768], P('dev'), may hold values from 0.2 to 2
- wind_dir: float32 [32768], P('dev'), may hold values from -3.140625 to 3.140625
- coupling: float32 [36, 36], replicated, may hold values from -1 to 1
- land_mask: int32 [96, 512], replicated, may hold values from 0 to 1, as said below
- sea_index: int32 [32768], replicated, may hold values from 0 to 49151, as said below
Outputs:
- updated: float32 [32768, 1296], P('dev')
The draws below stay inside these ranges and needn't reach their ends.
Inputs may be any that keep to these rules, and one draw needn't show every extreme that they name: land_mask is 1 at exactly the 32768 cells named in sea_index; land comes in blocks of 8 x 8 cells of mixed shares. sea_index holds 32768 different cells, the first and the last cell of the grid among them. With the sea cells in increasing order as s_0, s_1, ..., row d * 256 + i holds s_(i * 128 + d).
All inputs are finite; a program needn't handle non-finite values.
Results may differ from the reference program's by a relative error of at most 0.0003.
Values sent between devices are 32-bit elements; how exact they have to be, the bound alone decides.
No kernel may reach another device: no remote copies, remote signals or barrier semaphores. Data moves between devices by JAX's collectives and lax.ppermute only.
A program may use at most 320 MiB of HBM per device.

```python
import math
import jax
import jax.numpy as jnp
from jax import lax

NDIR = 36
NFREQ = 36
SUB = 4
P_DEV = 256
NYG = 512
BINS = 1296
SEA = 32768
NXG = 96
N_DEV = 128


def coast(key):
    cells = NXG * NYG
    block_key, rank_key = jax.random.split(key)
    coarse = jax.random.randint(block_key, (NXG // 8, NYG // 8), 0, 4)
    blocks = jnp.repeat(jnp.repeat(coarse, 8, axis=0), 8, axis=1).reshape(-1)
    ranks = jax.random.permutation(rank_key, cells)
    positions = jnp.arange(cells)
    corners = jnp.where((positions == 0) | (positions == cells - 1), 4 * cells, 0)
    scores = (blocks * cells + ranks + corners).astype(jnp.int32)
    values, chosen = lax.top_k(scores, SEA)
    ordered = jnp.sort(chosen).astype(jnp.int32)
    dealt = ordered.reshape(P_DEV, N_DEV).T.reshape(-1)
    seamask = jnp.zeros((cells,), jnp.int32).at[ordered].set(1).reshape(NXG, NYG)
    return (seamask, dealt)


def draw_land_mask(key, part):
    return coast(key)[0]


def draw_sea_index(key, part):
    return coast(key)[1]


def block_levels(own_key, extent, shards, low, high):
    loudness = 1.0
    for axis_at, shards_of in shards:
        draws = jax.random.uniform(jax.random.fold_in(jax.random.fold_in(own_key, 6), axis_at), (shards_of,), jnp.float32, low / len(shards), high / len(shards))
        loudness = loudness * jnp.repeat(jnp.exp(draws), extent[axis_at] // shards_of).reshape((-1,) + (1,) * (len(extent) - 1 - axis_at))
    return loudness


def noise(stream_key, dims, spread, limit, held_as=jnp.bfloat16):
    drawn = jax.random.normal(stream_key, dims, jnp.float32) * spread
    return jnp.minimum(jnp.maximum(drawn, -limit), limit).astype(held_as)


def setup_inputs(seed: int = 0) -> dict:
    key_of = jax.random.split(jax.random.key(seed), 7)
    return {
        "spectrum": jnp.clip(jnp.exp(math.log(2.0) - 5.2983174 * jax.random.uniform(key_of[0], (SEA, BINS), jnp.float32) ** block_levels(key_of[0], (SEA, BINS), ((0, 128),), -0.2, 0.2)), 0.01, 2.0),
        "wind_speed": jnp.clip(jnp.exp(math.log(2.0) - 2.3025851 * jax.random.uniform(key_of[1], (SEA,), jnp.float32) ** block_levels(key_of[1], (SEA,), ((0, 128),), -0.2, 0.2)), 0.2, 2.0),
        "wind_dir": jnp.clip(jax.random.uniform(key_of[2], (SEA,), jnp.float32, -3.140625, 3.140625), -3.140625, 3.140625),
        "coupling": noise(key_of[3], (NFREQ, NFREQ), NFREQ ** -0.5, 1.0, jnp.float32),
        "land_mask": draw_land_mask(jax.random.fold_in(key_of[6], 71), 0),
        "sea_index": draw_sea_index(jax.random.fold_in(key_of[6], 71), 0),
    }


def source_terms(spectrum, wind_speed, wind_dir, coupling):
    rows = spectrum.shape[0]
    angles = jnp.arange(NDIR).astype(jnp.float32) * (2.0 * jnp.pi / NDIR)
    phases = (jnp.arange(NFREQ).astype(jnp.float32) + 1.0) / NFREQ
    energy = lax.optimization_barrier(jnp.mean(spectrum, axis=1))
    shaped = spectrum.reshape(rows, NDIR, NFREQ)
    align = jnp.maximum(jnp.cos(angles[None, :] - wind_dir[:, None]), 0.0)
    growth = wind_speed[:, None, None] * align[:, :, None] * phases[None, None, :]
    damping = 0.5 * jnp.sqrt(energy / (energy + 1.0))[:, None, None] * phases[None, None, :]
    relaxed = shaped * jnp.exp(growth - damping)
    transfer = jnp.einsum('pdf,fg->pdg', relaxed, coupling, precision=lax.Precision.HIGHEST)
    return (relaxed + 0.2 * transfer).reshape(rows, NDIR * NFREQ)

def advect(fields, xspeed, yspeed, seamask):
    for step in range(SUB):
        low_x = jnp.pad(fields[:, :-1, :], ((0, 0), (1, 0), (0, 0)))
        high_x = jnp.pad(fields[:, 1:, :], ((0, 0), (0, 1), (0, 0)))
        low_y = jnp.pad(fields[:, :, :-1], ((0, 0), (0, 0), (1, 0)))
        high_y = jnp.pad(fields[:, :, 1:], ((0, 0), (0, 0), (0, 1)))
        upwind_x = jnp.where(xspeed > 0, low_x, high_x)
        upwind_y = jnp.where(yspeed > 0, low_y, high_y)
        fields = seamask * (fields - jnp.abs(xspeed) * (fields - upwind_x) - jnp.abs(yspeed) * (fields - upwind_y))
    return fields

def reference(spectrum, wind_speed, wind_dir, coupling, land_mask, sea_index):
    forced = source_terms(spectrum, wind_speed, wind_dir, coupling)
    nxg, nyg = land_mask.shape
    seamask = land_mask.astype(jnp.float32)[None]
    shaped = forced.reshape(forced.shape[0], NDIR, NFREQ)
    speeds = 0.45 * 1.1 ** (-jnp.arange(NFREQ).astype(jnp.float32))

    def one_direction(k):
        angle = k.astype(jnp.float32) * (2.0 * jnp.pi / NDIR)
        column = lax.dynamic_index_in_dim(shaped, k, 1, keepdims=False).T
        grid = jnp.zeros((NFREQ, nxg * nyg), jnp.float32).at[:, sea_index].set(column)
        xspeed = (speeds * jnp.cos(angle))[:, None, None]
        yspeed = (speeds * jnp.sin(angle))[:, None, None]
        moved = advect(grid.reshape(NFREQ, nxg, nyg), xspeed, yspeed, seamask)
        return moved.reshape(NFREQ, nxg * nyg)[:, sea_index]
    result = lax.map(one_direction, jnp.arange(NDIR).astype(jnp.int32))
    return result.reshape(NDIR * NFREQ, -1).T
```

```python
import jax
import jax.numpy as jnp
from jax import lax
from jax.experimental import pallas as pl
from jax.experimental.pallas import tpu as pltpu
from jax.sharding import PartitionSpec as P

NDIR = 36
NFREQ = 36
BINS = NDIR * NFREQ
SUB = 4
NXG = 96
NYG = 512
N_DEV = 128
P_DEV = 256
LANES = 128
COLS = NYG // LANES
BLOCKS = NXG * COLS
QUAD = BINS // 4
QDEV = N_DEV // 4
SLOTS = -(-QUAD // QDEV)
QPAD = SLOTS * QDEV
GROUP = 16
HALVES = P_DEV // LANES
CHUNK = SLOTS * HALVES
ROWS = N_DEV * CHUNK
PAIR = 2 * NFREQ
VMEM = 48 * 1024 * 1024


def source_kernel(spec_ref, speed_ref, dir_ref, coupling_ref, out_ref, amp_ref):
    f32 = jnp.float32
    energy = jnp.sum(spec_ref[...], axis=0, keepdims=True) * (1.0 / BINS)
    damp = 0.5 * jnp.sqrt(energy / (energy + 1.0))
    angles = lax.broadcasted_iota(jnp.int32, (40, P_DEV), 0).astype(f32) * (2.0 * jnp.pi / NDIR)
    align = jnp.maximum(jnp.cos(angles - dir_ref[...]), 0.0)
    amp_ref[...] = speed_ref[...] * align - damp

    row = lax.broadcasted_iota(jnp.int32, (PAIR, NFREQ), 0)
    col = lax.broadcasted_iota(jnp.int32, (PAIR, NFREQ), 1)
    spread = jnp.where(jnp.where(row >= NFREQ, row - NFREQ, row) == col, 1.0, 0.0).astype(f32)
    dims = (((1,), (1,)), ((), ()))
    best = lax.Precision.HIGHEST
    tall = lax.dot_general(spread, coupling_ref[...], dims, precision=best, preferred_element_type=f32)
    both = lax.dot_general(tall, spread, dims, precision=best, preferred_element_type=f32)
    at = lax.broadcasted_iota(jnp.int32, (PAIR, PAIR), 0) >= NFREQ
    to = lax.broadcasted_iota(jnp.int32, (PAIR, PAIR), 1) >= NFREQ
    matrix = jnp.where(at == to, 0.2 * both, 0.0)

    place = lax.broadcasted_iota(jnp.int32, (PAIR, P_DEV), 0)
    first = place < NFREQ
    phase = (jnp.where(first, place, place - NFREQ).astype(f32) + 1.0) * (1.0 / NFREQ)

    for quad in range(4):
        begin = 2 * (QPAD * quad + 320)
        out_ref[begin : begin + 64, :] = jnp.zeros((64, LANES), f32)

    for pair in range(NDIR // 2):
        low = amp_ref[2 * pair : 2 * pair + 1, :]
        high = amp_ref[2 * pair + 1 : 2 * pair + 2, :]
        relaxed = spec_ref[PAIR * pair : PAIR * pair + PAIR, :] * jnp.exp(phase * jnp.where(first, low, high))
        forced = relaxed + lax.dot_general(
            matrix, relaxed, (((1,), (0,)), ((), ())), precision=best, preferred_element_type=f32
        )
        quad_low, quad_high = (2 * pair) // 9, (2 * pair + 1) // 9
        base = PAIR * pair + (QPAD - QUAD) * quad_low
        for half in range(HALVES):
            part = forced[:, half * LANES : (half + 1) * LANES]
            if quad_low == quad_high:
                out_ref[pl.ds(2 * base + half, PAIR, stride=2), :] = part
            else:
                other = PAIR * pair + (QPAD - QUAD) * quad_high + 32
                out_ref[pl.ds(2 * base + half, 40, stride=2), :] = part[:40]
                out_ref[pl.ds(2 * other + half, 40, stride=2), :] = part[32:]


def source_terms(spectrum, wind_speed, wind_dir, coupling):
    return pl.pallas_call(
        source_kernel,
        out_shape=jax.ShapeDtypeStruct((ROWS, LANES), jnp.float32),
        in_specs=[pl.BlockSpec(memory_space=pltpu.VMEM)] * 4,
        out_specs=pl.BlockSpec(memory_space=pltpu.VMEM),
        scratch_shapes=[pltpu.VMEM((40, P_DEV), jnp.float32)],
        compiler_params=pltpu.CompilerParams(vmem_limit_bytes=VMEM),
        name="source_terms",
    )(spectrum.T, wind_speed.reshape(1, P_DEV), wind_dir.reshape(1, P_DEV), coupling)


def propagate_kernel(meta_ref, recv_ref, index_ref, mask_ref, spot_ref, coef_ref, out_ref, src, dst, *bufs):
    f32 = jnp.float32
    bufs = [bufs[2 * s : 2 * s + 2] for s in range(SUB + 1)]
    up_x = meta_ref[BLOCKS + 1]
    up_y = meta_ref[BLOCKS + 2]
    lane = lax.broadcasted_iota(jnp.int32, (GROUP, LANES), 1)
    edge = lane == jnp.where(up_y > 0, 0, LANES - 1)
    shift = jnp.where(up_y > 0, 1, LANES - 1)

    for slot in range(SLOTS):
        for half in range(HALVES):
            part = recv_ref[pl.ds(HALVES * slot + half, N_DEV, stride=CHUNK), :]
            src[pl.ds(half * LANES * GROUP + slot, LANES, stride=GROUP), :] = part.T

    for pair in bufs:
        for buf in pair:
            buf[...] = jnp.zeros_like(buf)

    coef_stay = coef_ref[0:GROUP, :]
    coef_x = coef_ref[GROUP : 2 * GROUP, :]
    coef_y = coef_ref[2 * GROUP : 3 * GROUP, :]

    def block(row, j):
        row = jnp.clip(row, 0, NXG - 1)
        g = jnp.where(up_x > 0, row, NXG - 1 - row)
        return g * COLS + jnp.where(up_y > 0, j, COLS - 1 - j)

    def at(j):
        return slice(j * GROUP, (j + 1) * GROUP)

    def advance(t, p):
        for j in range(COLS):
            cell = block(t - SUB - 1, j)
            start = meta_ref[cell]
            count = meta_ref[cell + 1] - start
            line = start >> 7
            off = start & (LANES - 1)
            one = jnp.broadcast_to(spot_ref[pl.ds(line, 1), :], (GROUP, LANES))
            two = jnp.broadcast_to(spot_ref[pl.ds(line + 1, 1), :], (GROUP, LANES))
            spots = jnp.where(lane >= off, one, two)
            taken = jnp.take_along_axis(bufs[SUB][1 - p][at(j), :], spots, axis=1, mode="promise_in_bounds")
            end = jnp.where(t - SUB - 1 < NXG, off + count, 0)
            here = pl.ds(pl.multiple_of(line * GROUP, GROUP), GROUP)
            after = pl.ds(pl.multiple_of((line + 1) * GROUP, GROUP), GROUP)
            pltpu.store(dst.at[here, :], taken, mask=(lane >= off) & (lane < end))
            pltpu.store(dst.at[after, :], taken, mask=lane < end - LANES)

        for step in range(SUB, 0, -1):
            fields = [bufs[step - 1][1 - p][at(j), :] for j in range(COLS)]
            turned = [pltpu.roll(field, shift, 1) for field in fields]
            for j in range(COLS):
                upwind_x = bufs[step - 1][p][at(j), :]
                upwind_y = jnp.where(edge, turned[j - 1] if j else 0.0, turned[j])
                sea = mask_ref[pl.ds(block(t - step, j), 1), :]
                moved = coef_stay * fields[j] + coef_x * upwind_x + coef_y * upwind_y
                bufs[step][p][at(j), :] = sea * moved

        for j in range(COLS):
            cell = block(t, j)
            start = meta_ref[cell]
            line = start >> 7
            off = start & (LANES - 1)
            one = src[pl.ds(pl.multiple_of(line * GROUP, GROUP), GROUP), :]
            two = src[pl.ds(pl.multiple_of((line + 1) * GROUP, GROUP), GROUP), :]
            index = jnp.broadcast_to(index_ref[pl.ds(cell, 1), :], (GROUP, LANES))
            placed = jnp.take_along_axis(jnp.where(lane >= off, one, two), index, axis=1, mode="promise_in_bounds")
            bufs[0][p][at(j), :] = jnp.where(mask_ref[pl.ds(cell, 1), :] > 0, placed, 0.0)

    def two_rows(u, carry):
        advance(2 * u, 0)
        advance(2 * u + 1, 1)
        return carry

    lax.fori_loop(0, (NXG + SUB + 2) // 2, two_rows, 0)

    for slot in range(SLOTS):
        for half in range(HALVES):
            part = dst[pl.ds(half * LANES * GROUP + slot, LANES, stride=GROUP), :]
            out_ref[pl.ds(HALVES * slot + half, N_DEV, stride=CHUNK), :] = part.T


def propagate(recv, land_mask, sea_index):
    f32 = jnp.float32
    dev = lax.axis_index("dev")
    quad = dev // QDEV
    within = (dev % QDEV) * SLOTS + jnp.arange(GROUP)
    bins = quad * QUAD + within
    real = (within < QUAD) & (jnp.arange(GROUP) < SLOTS)
    speeds = jnp.where(real, 0.45 * 1.1 ** (-(bins % NFREQ).astype(f32)), 0.0)
    angle = (bins // NFREQ).astype(f32) * (2.0 * jnp.pi / NDIR)
    abs_x = jnp.abs(speeds * jnp.cos(angle))
    abs_y = jnp.abs(speeds * jnp.sin(angle))
    coef = jnp.broadcast_to(jnp.concatenate([1.0 - abs_x - abs_y, abs_x, abs_y])[:, None], (3 * GROUP, LANES))
    up_x = ((quad == 0) | (quad == 3)).astype(jnp.int32)
    up_y = (quad < 2).astype(jnp.int32)

    mask = land_mask.reshape(BLOCKS, LANES).astype(f32)
    upto = jnp.dot(mask, jnp.triu(jnp.ones((LANES, LANES), f32)), preferred_element_type=f32)
    before = jnp.dot(jnp.tril(jnp.ones((BLOCKS, BLOCKS), f32), -1), upto[:, LANES - 1 :], preferred_element_type=f32)
    index = (before + upto - mask).astype(jnp.int32) & (LANES - 1)
    starts = before[:, 0].astype(jnp.int32)
    meta = jnp.concatenate([starts, jnp.array([N_DEV * P_DEV], jnp.int32), up_x[None], up_y[None]])
    spot = jnp.pad((sea_index & (LANES - 1)).reshape(N_DEV, P_DEV).T, ((0, 8), (0, 0)))

    return pl.pallas_call(
        propagate_kernel,
        out_shape=jax.ShapeDtypeStruct((ROWS, LANES), f32),
        in_specs=[pl.BlockSpec(memory_space=pltpu.SMEM)] + [pl.BlockSpec(memory_space=pltpu.VMEM)] * 5,
        out_specs=pl.BlockSpec(memory_space=pltpu.VMEM),
        scratch_shapes=[pltpu.VMEM(((P_DEV + 2) * GROUP, LANES), f32)] * 2
        + [pltpu.VMEM((COLS * GROUP, LANES), f32)] * (2 * (SUB + 1)),
        compiler_params=pltpu.CompilerParams(vmem_limit_bytes=VMEM),
        name="propagate",
    )(meta, recv, index, mask, spot, coef)


def collect_kernel(in_ref, out_ref):
    for quad in (1, 0, 3, 2):
        lead = 4 * (quad % 2)
        for half in range(HALVES):
            part = in_ref[pl.ds(2 * (QPAD * quad - lead) + half, QUAD + lead, stride=2), :]
            out_ref[QUAD * quad - lead : QUAD * (quad + 1), half * LANES : (half + 1) * LANES] = part


def collect(back):
    return pl.pallas_call(
        collect_kernel,
        out_shape=jax.ShapeDtypeStruct((BINS, P_DEV), jnp.float32),
        in_specs=[pl.BlockSpec(memory_space=pltpu.VMEM)],
        out_specs=pl.BlockSpec(memory_space=pltpu.VMEM),
        compiler_params=pltpu.CompilerParams(vmem_limit_bytes=VMEM),
        name="collect",
    )(back)


def exchange(rows):
    swapped = lax.all_to_all(rows.reshape(ROWS, 1, LANES), "dev", split_axis=0, concat_axis=0, tiled=True)
    return swapped.reshape(ROWS, LANES)


def on_device(spectrum, wind_speed, wind_dir, coupling, land_mask, sea_index):
    sent = source_terms(spectrum, wind_speed, wind_dir, coupling)
    moved = propagate(exchange(sent), land_mask, sea_index)
    return collect(exchange(moved)).T


def solution(mesh):
    in_specs = (P("dev", None), P("dev"), P("dev"), P(), P(), P())
    return jax.shard_map(on_device, mesh=mesh, in_specs=in_specs, out_specs=P("dev", None), check_vma=False)
```

```python
import jax
import jax.numpy as jnp
from jax import lax
from jax.experimental import pallas as pl
from jax.experimental.pallas import tpu as pltpu
from jax.sharding import PartitionSpec as P

NDIR = 36
NFREQ = 36
BINS = NDIR * NFREQ
SUB = 4
NXG = 96
NYG = 512
N_DEV = 128
P_DEV = 256
LANES = 128
COLS = NYG // LANES
BLOCKS = NXG * COLS
QUAD = BINS // 4
QDEV = N_DEV // 4
SLOTS = -(-QUAD // QDEV)
QPAD = SLOTS * QDEV
GROUP = 16
HALVES = P_DEV // LANES
CHUNK = SLOTS * HALVES
ROWS = N_DEV * CHUNK
PAIR = 2 * NFREQ
PARTS = 6
PART = BINS // PARTS
SLAB = 2
SLABS = NXG // SLAB
STEP = SLAB * COLS
MERGE_OUT = False
DELAY = SUB if MERGE_OUT else SUB + 1
ROUNDS = -(-(SLABS + DELAY) // 2) * 2
ALONG_LANES = lax.GatherDimensionNumbers(
    offset_dims=(),
    collapsed_slice_dims=(1,),
    start_index_map=(1,),
    operand_batching_dims=(0,),
    start_indices_batching_dims=(0,),
)
VMEM = 48 * 1024 * 1024


def source_kernel(spec_hbm, speed_hbm, dir_hbm, coupling_hbm, out_hbm, spec, speed, dirs, coupling, amp, out, in_sems, out_sems):
    f32 = jnp.float32
    small = [
        pltpu.make_async_copy(source, target, in_sems.at[PARTS + at])
        for at, (source, target) in enumerate(((speed_hbm, speed), (dir_hbm, dirs), (coupling_hbm, coupling)))
    ]
    loads = [
        pltpu.make_async_copy(spec_hbm.at[part, :], spec.at[part, :], in_sems.at[at])
        for at, part in enumerate(pl.ds(at * PART, PART) for at in range(PARTS))
    ]
    for copy in small + loads:
        copy.start()
    for copy in small:
        copy.wait()

    row = lax.broadcasted_iota(jnp.int32, (PAIR, NFREQ), 0)
    col = lax.broadcasted_iota(jnp.int32, (PAIR, NFREQ), 1)
    spread = jnp.where(jnp.where(row >= NFREQ, row - NFREQ, row) == col, 1.0, 0.0).astype(f32)
    dims = (((1,), (1,)), ((), ()))
    best = lax.Precision.HIGHEST
    tall = lax.dot_general(spread, coupling[...], dims, precision=best, preferred_element_type=f32)
    both = lax.dot_general(tall, spread, dims, precision=best, preferred_element_type=f32)
    at = lax.broadcasted_iota(jnp.int32, (PAIR, PAIR), 0) >= NFREQ
    to = lax.broadcasted_iota(jnp.int32, (PAIR, PAIR), 1) >= NFREQ
    matrix = jnp.where(at == to, 0.2 * both, 0.0)

    angles = lax.broadcasted_iota(jnp.int32, (40, P_DEV), 0).astype(f32) * (2.0 * jnp.pi / NDIR)
    align = jnp.maximum(jnp.cos(angles - dirs[...]), 0.0)
    growth = speed[...] * align

    place = lax.broadcasted_iota(jnp.int32, (PAIR, P_DEV), 0)
    first = place < NFREQ
    phase = (jnp.where(first, place, place - NFREQ).astype(f32) + 1.0) * (1.0 / NFREQ)

    for quad in range(4):
        begin = 2 * (QPAD * quad + 320)
        out[begin : begin + 64, :] = jnp.zeros((64, LANES), f32)

    total = jnp.zeros((8, P_DEV), f32)
    for at, copy in enumerate(loads):
        copy.wait()
        for tile in range(PART // 8):
            begin = at * PART + tile * 8
            total = total + spec[begin : begin + 8, :]
    energy = jnp.sum(total, axis=0, keepdims=True) * (1.0 / BINS)
    amp[...] = growth - 0.5 * jnp.sqrt(energy / (energy + 1.0))

    stores = []
    for pair in range(NDIR // 2):
        low = amp[2 * pair : 2 * pair + 1, :]
        high = amp[2 * pair + 1 : 2 * pair + 2, :]
        relaxed = spec[PAIR * pair : PAIR * pair + PAIR, :] * jnp.exp(phase * jnp.where(first, low, high))
        forced = relaxed + lax.dot_general(
            matrix, relaxed, (((1,), (0,)), ((), ())), precision=lax.Precision.HIGH, preferred_element_type=f32
        )
        quad_low, quad_high = (2 * pair) // 9, (2 * pair + 1) // 9
        base = PAIR * pair + (QPAD - QUAD) * quad_low
        for half in range(HALVES):
            part = forced[:, half * LANES : (half + 1) * LANES]
            if quad_low == quad_high:
                out[pl.ds(2 * base + half, PAIR, stride=2), :] = part
            else:
                other = PAIR * pair + (QPAD - QUAD) * quad_high + 32
                out[pl.ds(2 * base + half, 40, stride=2), :] = part[:40]
                out[pl.ds(2 * other + half, 40, stride=2), :] = part[32:]
        if (2 * pair + 2) // 9 > len(stores):
            rows = pl.ds(len(stores) * 2 * QPAD, 2 * QPAD)
            stores.append(pltpu.make_async_copy(out.at[rows, :], out_hbm.at[rows, :], out_sems.at[len(stores)]))
            stores[-1].start()
    for copy in stores:
        copy.wait()


def source_terms(spectrum, wind_speed, wind_dir, coupling):
    f32 = jnp.float32
    return pl.pallas_call(
        source_kernel,
        out_shape=jax.ShapeDtypeStruct((ROWS, LANES), f32),
        in_specs=[pl.BlockSpec(memory_space=pltpu.HBM)] * 4,
        out_specs=pl.BlockSpec(memory_space=pltpu.HBM),
        scratch_shapes=[
            pltpu.VMEM((BINS, P_DEV), f32),
            pltpu.VMEM((1, P_DEV), f32),
            pltpu.VMEM((1, P_DEV), f32),
            pltpu.VMEM((NFREQ, NFREQ), f32),
            pltpu.VMEM((40, P_DEV), f32),
            pltpu.VMEM((ROWS, LANES), f32),
            pltpu.SemaphoreType.DMA((PARTS + 3,)),
            pltpu.SemaphoreType.DMA((4,)),
        ],
        compiler_params=pltpu.CompilerParams(vmem_limit_bytes=63 * 1024 * 1024),
        name="source_terms",
    )(spectrum.T, wind_speed.reshape(1, P_DEV), wind_dir.reshape(1, P_DEV), coupling)


def propagate_kernel(line_ref, off_ref, end_ref, up_ref, scale_ref, recv_ref, index_ref, mask_ref, spot_ref, coef_ref, out_ref, src, dst, *bufs):
    up_y = up_ref[0]
    lane = lax.broadcasted_iota(jnp.int32, (GROUP, LANES), 1)
    edge = lane == jnp.where(up_y > 0, 0, LANES - 1)
    shift = jnp.where(up_y > 0, 1, LANES - 1)

    for slot in range(SLOTS):
        for half in range(HALVES):
            part = recv_ref[pl.ds(HALVES * slot + half, N_DEV, stride=CHUNK), :]
            src[pl.ds(half * LANES * GROUP + slot, LANES, stride=GROUP), :] = part.T * scale_ref[slot]

    for buf in bufs:
        buf[...] = jnp.zeros_like(buf)
    bufs = [bufs[2 * s : 2 * s + 2] for s in range(SUB + 1)]

    coef_x = coef_ref[0:GROUP, :]
    coef_y = coef_ref[GROUP : 2 * GROUP, :]

    def wide(ref, cell):
        return jnp.broadcast_to(ref[pl.ds(cell, 1), :], (GROUP, LANES))

    def take(values, spots):
        return lax.gather(
            values, spots[:, :, None], ALONG_LANES, slice_sizes=(1, 1), mode=lax.GatherScatterMode.PROMISE_IN_BOUNDS
        )

    def lines(begin):
        return pl.ds(pl.multiple_of(begin, GROUP), GROUP)

    def at(i, j):
        begin = (i * COLS + j) * GROUP
        return slice(begin, begin + GROUP)

    def scatter(cell, values):
        taken = take(values, wide(spot_ref, cell))
        begin = line_ref[cell]
        off = off_ref[cell]
        end = end_ref[cell]
        pltpu.store(dst.at[lines(begin), :], taken, mask=(lane >= off) & (lane < end))
        pltpu.store(dst.at[lines(begin + GROUP), :], taken, mask=lane < end - LANES)

    def gather(cell):
        begin = line_ref[cell]
        both = jnp.where(lane >= off_ref[cell], src[lines(begin), :], src[lines(begin + GROUP), :])
        return jnp.where(wide(mask_ref, cell) > 0, take(both, wide(index_ref, cell)), 0.0)

    def round_of(u, p):
        base = pl.multiple_of(u * STEP, STEP)
        above = [[bufs[step][p][at(SLAB - 1, j), :] for j in range(COLS)] for step in range(SUB)]
        for i in range(SLAB):
            if not MERGE_OUT:
                for j in range(COLS):
                    scatter(base + (i * COLS + j), bufs[SUB][1 - p][at(i, j), :])
            for step in range(SUB, 0, -1):
                fields = [bufs[step - 1][1 - p][at(i, j), :] for j in range(COLS)]
                turned = [pltpu.roll(field, shift, 1) for field in fields]
                for j in range(COLS):
                    cell = base + ((DELAY - step) * STEP + i * COLS + j)
                    upwind_y = jnp.where(edge, turned[j - 1] if j else 0.0, turned[j])
                    moved = fields[j] + (coef_x * above[step - 1][j] + coef_y * upwind_y)
                    moved = wide(mask_ref, cell) * moved
                    if step == SUB and MERGE_OUT:
                        scatter(cell, moved)
                    else:
                        bufs[step][p][at(i, j), :] = moved
                above[step - 1] = fields
            for j in range(COLS):
                bufs[0][p][at(i, j), :] = gather(base + (DELAY * STEP + i * COLS + j))

    def two_rounds(u, carry):
        round_of(2 * u, 0)
        round_of(2 * u + 1, 1)
        return carry

    lax.fori_loop(0, ROUNDS // 2, two_rounds, 0, unroll=3)

    for slot in range(SLOTS):
        for half in range(HALVES):
            part = dst[pl.ds(half * LANES * GROUP + slot, LANES, stride=GROUP), :]
            out_ref[pl.ds(HALVES * slot + half, N_DEV, stride=CHUNK), :] = part.T


def propagation_tables(land_mask, sea_index):
    f32 = jnp.float32
    dev = lax.axis_index("dev")
    quad = dev // QDEV
    within = (dev % QDEV) * SLOTS + jnp.arange(GROUP)
    bins = quad * QUAD + within
    real = (within < QUAD) & (jnp.arange(GROUP) < SLOTS)
    speeds = jnp.where(real, 0.45 * 1.1 ** (-(bins % NFREQ).astype(f32)), 0.0)
    angle = (bins // NFREQ).astype(f32) * (2.0 * jnp.pi / NDIR)
    abs_x = jnp.abs(speeds * jnp.cos(angle))
    abs_y = jnp.abs(speeds * jnp.sin(angle))
    stay = 1.0 - abs_x - abs_y
    coef = jnp.broadcast_to(jnp.concatenate([abs_x / stay, abs_y / stay])[:, None], (2 * GROUP, LANES))
    scale = stay * stay * stay * stay
    up_x = (quad == 0) | (quad == 3)
    up_y = quad < 2

    def ordered(table):
        table = table.reshape((NXG, COLS) + table.shape[1:])
        table = jnp.where(up_x, table, jnp.flip(table, 0))
        table = jnp.where(up_y, table, jnp.flip(table, 1))
        table = table.reshape((BLOCKS,) + table.shape[2:])
        return jnp.pad(table, ((DELAY * STEP, (ROUNDS - SLABS) * STEP),) + ((0, 0),) * (table.ndim - 1))

    mask = land_mask.reshape(BLOCKS, LANES).astype(f32)
    upto = jnp.dot(mask, jnp.triu(jnp.ones((LANES, LANES), f32)), preferred_element_type=f32)
    before = jnp.dot(jnp.tril(jnp.ones((BLOCKS, BLOCKS), f32), -1), upto[:, LANES - 1 :], preferred_element_type=f32)
    index = (before + upto - mask).astype(jnp.int32) & (LANES - 1)
    start = before[:, 0].astype(jnp.int32)
    line = start >> 7
    off = start & (LANES - 1)
    end = off + upto[:, LANES - 1].astype(jnp.int32)

    spot = (sea_index & (LANES - 1)).reshape(N_DEV, P_DEV).T.astype(f32)
    lines = jnp.arange(P_DEV)
    one = jnp.dot((line[:, None] == lines).astype(f32), spot, preferred_element_type=f32)
    two = jnp.dot((line[:, None] + 1 == lines).astype(f32), spot, preferred_element_type=f32)
    spots = jnp.where(jnp.arange(LANES) >= off[:, None], one, two).astype(jnp.int32)

    scalars = [ordered(line * GROUP), ordered(off), ordered(end), up_y.astype(jnp.int32)[None], scale]
    return scalars, [ordered(index), ordered(mask), ordered(spots), coef]


def propagate(recv, scalars, vectors):
    f32 = jnp.float32
    return pl.pallas_call(
        propagate_kernel,
        out_shape=jax.ShapeDtypeStruct((ROWS, LANES), f32),
        in_specs=[pl.BlockSpec(memory_space=pltpu.SMEM)] * 5 + [pl.BlockSpec(memory_space=pltpu.VMEM)] * 5,
        out_specs=pl.BlockSpec(memory_space=pltpu.VMEM),
        scratch_shapes=[pltpu.VMEM(((P_DEV + 2) * GROUP, LANES), f32)] * 2
        + [pltpu.VMEM((SLAB * COLS * GROUP, LANES), f32)] * (2 * (SUB + 1)),
        compiler_params=pltpu.CompilerParams(vmem_limit_bytes=VMEM),
        name="propagate",
    )(*scalars, recv, *vectors)


def collect_kernel(in_ref, out_ref):
    for quad in (1, 0, 3, 2):
        lead = 4 * (quad % 2)
        for half in range(HALVES):
            part = in_ref[pl.ds(2 * (QPAD * quad - lead) + half, QUAD + lead, stride=2), :]
            out_ref[QUAD * quad - lead : QUAD * (quad + 1), half * LANES : (half + 1) * LANES] = part


def collect(back):
    return pl.pallas_call(
        collect_kernel,
        out_shape=jax.ShapeDtypeStruct((BINS, P_DEV), jnp.float32),
        in_specs=[pl.BlockSpec(memory_space=pltpu.VMEM)],
        out_specs=pl.BlockSpec(memory_space=pltpu.VMEM),
        compiler_params=pltpu.CompilerParams(vmem_limit_bytes=VMEM),
        name="collect",
    )(back)


def exchange(rows):
    swapped = lax.all_to_all(rows.reshape(ROWS, 1, LANES), "dev", split_axis=0, concat_axis=0, tiled=True)
    return swapped.reshape(ROWS, LANES)


def on_device(spectrum, wind_speed, wind_dir, coupling, land_mask, sea_index):
    sent = source_terms(spectrum, wind_speed, wind_dir, coupling)
    moved = propagate(exchange(sent), *propagation_tables(land_mask, sea_index))
    return collect(exchange(moved)).T


def solution(mesh):
    in_specs = (P("dev", None), P("dev"), P("dev"), P(), P(), P())
    return jax.shard_map(on_device, mesh=mesh, in_specs=in_specs, out_specs=P("dev", None), check_vma=False)
```

```python
import jax
import jax.numpy as jnp
from jax import lax
from jax.experimental import pallas as pl
from jax.experimental.pallas import tpu as pltpu
from jax.sharding import PartitionSpec as P

NDIR = 36
NFREQ = 36
BINS = NDIR * NFREQ
SUB = 4
NXG = 96
NYG = 512
N_DEV = 128
P_DEV = 256
LANES = 128
COLS = NYG // LANES
BLOCKS = NXG * COLS
QUAD = BINS // 4
QDEV = N_DEV // 4
SLOTS = QUAD // QDEV
REST = QUAD - SLOTS * QDEV
WINDOWS = 3
OWNED = (0, 100, 160, 256)
GROUP = 16
HALVES = P_DEV // LANES
CHUNK = SLOTS * HALVES + 1
ROWS = N_DEV * CHUNK
PAIR = 2 * NFREQ
PARTS = 6
PART = BINS // PARTS
SLAB = 2
SLABS = NXG // SLAB
STEP = SLAB * COLS
MERGE_OUT = False
DELAY = SUB if MERGE_OUT else SUB + 1
ROUNDS = -(-(SLABS + DELAY) // 2) * 2
ALONG_LANES = lax.GatherDimensionNumbers(
    offset_dims=(),
    collapsed_slice_dims=(1,),
    start_index_map=(1,),
    operand_batching_dims=(0,),
    start_indices_batching_dims=(0,),
)
VMEM = 48 * 1024 * 1024


def first_bin(quad):
    return QUAD * quad + REST * (quad % 2)


def source_kernel(spec_hbm, speed_hbm, dir_hbm, coupling_hbm, out_hbm, spec, speed, dirs, coupling, amp, out, in_sems, out_sems):
    f32 = jnp.float32
    small = [
        pltpu.make_async_copy(source, target, in_sems.at[PARTS + at])
        for at, (source, target) in enumerate(((speed_hbm, speed), (dir_hbm, dirs), (coupling_hbm, coupling)))
    ]
    loads = [
        pltpu.make_async_copy(spec_hbm.at[part, :], spec.at[part, :], in_sems.at[at])
        for at, part in enumerate(pl.ds(at * PART, PART) for at in range(PARTS))
    ]
    for copy in small + loads:
        copy.start()
    for copy in small:
        copy.wait()

    row = lax.broadcasted_iota(jnp.int32, (PAIR, NFREQ), 0)
    col = lax.broadcasted_iota(jnp.int32, (PAIR, NFREQ), 1)
    spread = jnp.where(jnp.where(row >= NFREQ, row - NFREQ, row) == col, 1.0, 0.0).astype(f32)
    dims = (((1,), (1,)), ((), ()))
    best = lax.Precision.HIGHEST
    tall = lax.dot_general(spread, coupling[...], dims, precision=best, preferred_element_type=f32)
    both = lax.dot_general(tall, spread, dims, precision=best, preferred_element_type=f32)
    at = lax.broadcasted_iota(jnp.int32, (PAIR, PAIR), 0) >= NFREQ
    to = lax.broadcasted_iota(jnp.int32, (PAIR, PAIR), 1) >= NFREQ
    matrix = jnp.where(at == to, 0.2 * both, 0.0)

    angles = lax.broadcasted_iota(jnp.int32, (40, P_DEV), 0).astype(f32) * (2.0 * jnp.pi / NDIR)
    align = jnp.maximum(jnp.cos(angles - dirs[...]), 0.0)
    growth = speed[...] * align

    place = lax.broadcasted_iota(jnp.int32, (PAIR, P_DEV), 0)
    first = place < NFREQ
    phase = (jnp.where(first, place, place - NFREQ).astype(f32) + 1.0) * (1.0 / NFREQ)

    lane = lax.broadcasted_iota(jnp.int32, (8, LANES), 1)
    unused = QDEV - REST * WINDOWS
    for quad in range(4):
        begin = (QDEV * (quad + 1) - unused) * CHUNK + CHUNK - 1
        out[pl.ds(begin, unused, stride=CHUNK), :] = jnp.zeros((unused, LANES), f32)

    total = jnp.zeros((8, P_DEV), f32)
    for at, copy in enumerate(loads):
        copy.wait()
        for tile in range(PART // 8):
            begin = at * PART + tile * 8
            total = total + spec[begin : begin + 8, :]
    energy = jnp.sum(total, axis=0, keepdims=True) * (1.0 / BINS)
    amp[...] = growth - 0.5 * jnp.sqrt(energy / (energy + 1.0))

    stores = []
    for pair in range(NDIR // 2):
        low = amp[2 * pair : 2 * pair + 1, :]
        high = amp[2 * pair + 1 : 2 * pair + 2, :]
        relaxed = spec[PAIR * pair : PAIR * pair + PAIR, :] * jnp.exp(phase * jnp.where(first, low, high))
        forced = relaxed + lax.dot_general(
            matrix, relaxed, (((1,), (0,)), ((), ())), precision=lax.Precision.HIGH, preferred_element_type=f32
        )
        for tile in range(PAIR // 8):
            begin = PAIR * pair + tile * 8
            halves = [forced[tile * 8 : tile * 8 + 8, half * LANES : (half + 1) * LANES] for half in range(HALVES)]
            if begin % (2 * QUAD) == QUAD - REST:
                turned = [pltpu.roll(half, LANES // 2, 1) for half in halves]
                windows = (halves[0], jnp.where(lane < LANES // 2, turned[0], turned[1]), halves[1])
                for at in range(2):
                    for window in range(WINDOWS):
                        first_row = ((begin // QUAD + at) * QDEV + window) * CHUNK + CHUNK - 1
                        rows = pl.ds(first_row, REST, stride=WINDOWS * CHUNK)
                        out[rows, :] = windows[window][at * REST : (at + 1) * REST]
            else:
                quad = begin // QUAD
                slot, member = divmod(begin - first_bin(quad), QDEV)
                for half in range(HALVES):
                    first_row = (quad * QDEV + member) * CHUNK + HALVES * slot + half
                    out[pl.ds(first_row, 8, stride=CHUNK), :] = halves[half]
        if (2 * pair + 2) // 9 > len(stores):
            rows = pl.ds(len(stores) * QDEV * CHUNK, QDEV * CHUNK)
            stores.append(pltpu.make_async_copy(out.at[rows, :], out_hbm.at[rows, :], out_sems.at[len(stores)]))
            stores[-1].start()
    for copy in stores:
        copy.wait()


def source_terms(spectrum, wind_speed, wind_dir, coupling):
    f32 = jnp.float32
    return pl.pallas_call(
        source_kernel,
        out_shape=jax.ShapeDtypeStruct((ROWS, LANES), f32),
        in_specs=[pl.BlockSpec(memory_space=pltpu.HBM)] * 4,
        out_specs=pl.BlockSpec(memory_space=pltpu.HBM),
        scratch_shapes=[
            pltpu.VMEM((BINS, P_DEV), f32),
            pltpu.VMEM((1, P_DEV), f32),
            pltpu.VMEM((1, P_DEV), f32),
            pltpu.VMEM((NFREQ, NFREQ), f32),
            pltpu.VMEM((40, P_DEV), f32),
            pltpu.VMEM((ROWS, LANES), f32),
            pltpu.SemaphoreType.DMA((PARTS + 3,)),
            pltpu.SemaphoreType.DMA((4,)),
        ],
        compiler_params=pltpu.CompilerParams(vmem_limit_bytes=63 * 1024 * 1024),
        name="source_terms",
    )(spectrum.T, wind_speed.reshape(1, P_DEV), wind_dir.reshape(1, P_DEV), coupling)


def propagate_kernel(line_ref, off_ref, end_ref, up_ref, scale_ref, recv_ref, index_ref, mask_ref, spot_ref, coef_ref, out_ref, src, dst, *bufs):
    up_y = up_ref[0]
    lane = lax.broadcasted_iota(jnp.int32, (GROUP, LANES), 1)
    edge = lane == jnp.where(up_y > 0, 0, LANES - 1)
    shift = jnp.where(up_y > 0, 1, LANES - 1)

    pieces = [(HALVES * slot + half, slot, half * LANES * GROUP) for slot in range(SLOTS) for half in range(HALVES)]
    pieces.append((CHUNK - 1, SLOTS, up_ref[1] * (LANES // 2 * GROUP)))
    for row, slot, begin in pieces:
        part = recv_ref[pl.ds(row, N_DEV, stride=CHUNK), :]
        src[pl.ds(begin + slot, LANES, stride=GROUP), :] = part.T * scale_ref[slot]

    for buf in bufs:
        buf[...] = jnp.zeros_like(buf)
    bufs = [bufs[2 * s : 2 * s + 2] for s in range(SUB + 1)]

    coef_x = coef_ref[0:GROUP, :]
    coef_y = coef_ref[GROUP : 2 * GROUP, :]

    def wide(ref, cell):
        return jnp.broadcast_to(ref[pl.ds(cell, 1), :], (GROUP, LANES))

    def take(values, spots):
        return lax.gather(
            values, spots[:, :, None], ALONG_LANES, slice_sizes=(1, 1), mode=lax.GatherScatterMode.PROMISE_IN_BOUNDS
        )

    def lines(begin):
        return pl.ds(pl.multiple_of(begin, GROUP), GROUP)

    def at(i, j):
        begin = (i * COLS + j) * GROUP
        return slice(begin, begin + GROUP)

    def scatter(cell, values):
        taken = take(values, wide(spot_ref, cell))
        begin = line_ref[cell]
        off = off_ref[cell]
        end = end_ref[cell]
        pltpu.store(dst.at[lines(begin), :], taken, mask=(lane >= off) & (lane < end))
        pltpu.store(dst.at[lines(begin + GROUP), :], taken, mask=lane < end - LANES)

    def gather(cell):
        begin = line_ref[cell]
        both = jnp.where(lane >= off_ref[cell], src[lines(begin), :], src[lines(begin + GROUP), :])
        return jnp.where(wide(mask_ref, cell) > 0, take(both, wide(index_ref, cell)), 0.0)

    def round_of(u, p):
        base = pl.multiple_of(u * STEP, STEP)
        above = [[bufs[step][p][at(SLAB - 1, j), :] for j in range(COLS)] for step in range(SUB)]
        for i in range(SLAB):
            if not MERGE_OUT:
                for j in range(COLS):
                    scatter(base + (i * COLS + j), bufs[SUB][1 - p][at(i, j), :])
            for step in range(SUB, 0, -1):
                fields = [bufs[step - 1][1 - p][at(i, j), :] for j in range(COLS)]
                turned = [pltpu.roll(field, shift, 1) for field in fields]
                for j in range(COLS):
                    cell = base + ((DELAY - step) * STEP + i * COLS + j)
                    upwind_y = jnp.where(edge, turned[j - 1] if j else 0.0, turned[j])
                    moved = fields[j] + (coef_x * above[step - 1][j] + coef_y * upwind_y)
                    moved = wide(mask_ref, cell) * moved
                    if step == SUB and MERGE_OUT:
                        scatter(cell, moved)
                    else:
                        bufs[step][p][at(i, j), :] = moved
                above[step - 1] = fields
            for j in range(COLS):
                bufs[0][p][at(i, j), :] = gather(base + (DELAY * STEP + i * COLS + j))

    def two_rounds(u, carry):
        round_of(2 * u, 0)
        round_of(2 * u + 1, 1)
        return carry

    lax.fori_loop(0, ROUNDS // 2, two_rounds, 0, unroll=3)

    for row, slot, begin in pieces:
        part = dst[pl.ds(begin + slot, LANES, stride=GROUP), :]
        out_ref[pl.ds(row, N_DEV, stride=CHUNK), :] = part.T


def propagation_tables(land_mask, sea_index):
    f32 = jnp.float32
    dev = lax.axis_index("dev")
    quad = dev // QDEV
    member = dev % QDEV
    slots = jnp.arange(GROUP)
    odd = quad % 2
    whole = quad * QUAD + REST * odd + QDEV * slots + member
    rest = quad * QUAD + (QUAD - REST) * (1 - odd) + member // WINDOWS
    bins = jnp.where(slots < SLOTS, whole, rest)
    real = (slots < SLOTS) | ((slots == SLOTS) & (member < REST * WINDOWS))
    speeds = jnp.where(real, 0.45 * 1.1 ** (-(bins % NFREQ).astype(f32)), 0.0)
    angle = (bins // NFREQ).astype(f32) * (2.0 * jnp.pi / NDIR)
    abs_x = jnp.abs(speeds * jnp.cos(angle))
    abs_y = jnp.abs(speeds * jnp.sin(angle))
    stay = 1.0 - abs_x - abs_y
    coef = jnp.broadcast_to(jnp.concatenate([abs_x / stay, abs_y / stay])[:, None], (2 * GROUP, LANES))
    scale = stay * stay * stay * stay
    up_x = (quad == 0) | (quad == 3)
    up_y = quad < 2

    def ordered(table):
        table = table.reshape((NXG, COLS) + table.shape[1:])
        table = jnp.where(up_x, table, jnp.flip(table, 0))
        table = jnp.where(up_y, table, jnp.flip(table, 1))
        table = table.reshape((BLOCKS,) + table.shape[2:])
        return jnp.pad(table, ((DELAY * STEP, (ROUNDS - SLABS) * STEP),) + ((0, 0),) * (table.ndim - 1))

    mask = land_mask.reshape(BLOCKS, LANES).astype(f32)
    upto = jnp.dot(mask, jnp.triu(jnp.ones((LANES, LANES), f32)), preferred_element_type=f32)
    before = jnp.dot(jnp.tril(jnp.ones((BLOCKS, BLOCKS), f32), -1), upto[:, LANES - 1 :], preferred_element_type=f32)
    index = (before + upto - mask).astype(jnp.int32) & (LANES - 1)
    start = before[:, 0].astype(jnp.int32)
    line = start >> 7
    off = start & (LANES - 1)
    end = off + upto[:, LANES - 1].astype(jnp.int32)

    spot = (sea_index & (LANES - 1)).reshape(N_DEV, P_DEV).T.astype(f32)
    lines = jnp.arange(P_DEV)
    one = jnp.dot((line[:, None] == lines).astype(f32), spot, preferred_element_type=f32)
    two = jnp.dot((line[:, None] + 1 == lines).astype(f32), spot, preferred_element_type=f32)
    spots = jnp.where(jnp.arange(LANES) >= off[:, None], one, two).astype(jnp.int32)

    scalars = [ordered(line * GROUP), ordered(off), ordered(end), jnp.stack([up_y.astype(jnp.int32), member % WINDOWS]), scale]
    return scalars, [ordered(index), ordered(mask), ordered(spots), coef]


def propagate(recv, scalars, vectors):
    f32 = jnp.float32
    return pl.pallas_call(
        propagate_kernel,
        out_shape=jax.ShapeDtypeStruct((ROWS, LANES), f32),
        in_specs=[pl.BlockSpec(memory_space=pltpu.SMEM)] * 5 + [pl.BlockSpec(memory_space=pltpu.VMEM)] * 5,
        out_specs=pl.BlockSpec(memory_space=pltpu.VMEM),
        scratch_shapes=[pltpu.VMEM(((P_DEV + 2) * GROUP, LANES), f32)] * 2
        + [pltpu.VMEM((SLAB * COLS * GROUP, LANES), f32)] * (2 * (SUB + 1)),
        compiler_params=pltpu.CompilerParams(vmem_limit_bytes=VMEM),
        name="propagate",
    )(*scalars, recv, *vectors)


def collect_kernel(in_ref, out_ref):
    lane = lax.broadcasted_iota(jnp.int32, (REST, LANES), 1)
    for quad in range(4):
        for half in range(HALVES):
            columns = slice(half * LANES, (half + 1) * LANES)
            for slot in range(SLOTS):
                part = in_ref[pl.ds(quad * QDEV * CHUNK + HALVES * slot + half, QDEV, stride=CHUNK), :]
                begin = first_bin(quad) + QDEV * slot
                out_ref[begin : begin + QDEV, columns] = part
        begin = QUAD * quad + (0 if quad % 2 else QUAD - REST)
        low, middle, high = [
            in_ref[pl.ds((quad * QDEV + window) * CHUNK + CHUNK - 1, REST, stride=WINDOWS * CHUNK), :]
            for window in range(WINDOWS)
        ]
        middle = pltpu.roll(middle, LANES // 2, 1)
        out_ref[begin : begin + REST, :LANES] = jnp.where(lane < OWNED[1], low, middle)
        out_ref[begin : begin + REST, LANES:] = jnp.where(lane < OWNED[2] - LANES, middle, high)


def collect(back):
    return pl.pallas_call(
        collect_kernel,
        out_shape=jax.ShapeDtypeStruct((BINS, P_DEV), jnp.float32),
        in_specs=[pl.BlockSpec(memory_space=pltpu.VMEM)],
        out_specs=pl.BlockSpec(memory_space=pltpu.VMEM),
        compiler_params=pltpu.CompilerParams(vmem_limit_bytes=VMEM),
        name="collect",
    )(back)


def exchange(rows):
    swapped = lax.all_to_all(rows.reshape(ROWS, 1, LANES), "dev", split_axis=0, concat_axis=0, tiled=True)
    return swapped.reshape(ROWS, LANES)


def on_device(spectrum, wind_speed, wind_dir, coupling, land_mask, sea_index):
    sent = source_terms(spectrum, wind_speed, wind_dir, coupling)
    moved = propagate(exchange(sent), *propagation_tables(land_mask, sea_index))
    return collect(exchange(moved)).T


def solution(mesh):
    in_specs = (P("dev", None), P("dev"), P("dev"), P(), P(), P())
    return jax.shard_map(on_device, mesh=mesh, in_specs=in_specs, out_specs=P("dev", None), check_vma=False)
```

```python
import jax
import jax.numpy as jnp
from jax import lax
from jax.experimental import pallas as pl
from jax.experimental.pallas import tpu as pltpu
from jax.sharding import PartitionSpec as P

NDIR = 36
NFREQ = 36
BINS = NDIR * NFREQ
SUB = 4
NXG = 96
NYG = 512
N_DEV = 128
P_DEV = 256
LANES = 128
COLS = NYG // LANES
BLOCKS = NXG * COLS
QUAD = BINS // 4
QDEV = N_DEV // 4
SLOTS = QUAD // QDEV
REST = QUAD - SLOTS * QDEV
WINDOWS = 3
OWNED = (0, 100, 160, 256)
GROUP = 8
HALF = GROUP // 2
HELD = 2 * GROUP
HALVES = P_DEV // LANES
CHUNK = SLOTS * HALVES + 1
ROWS = N_DEV * CHUNK
PAIR = 2 * NFREQ
PARTS = 6
PART = BINS // PARTS
SLAB = 2
SLABS = NXG // SLAB
STEP = SLAB * COLS
UNROLL = 14
ALONG_LANES = lax.GatherDimensionNumbers(
    offset_dims=(),
    collapsed_slice_dims=(1,),
    start_index_map=(1,),
    operand_batching_dims=(0,),
    start_indices_batching_dims=(0,),
)
VMEM = 48 * 1024 * 1024


def first_bin(quad):
    return QUAD * quad + REST * (quad % 2)


def source_kernel(spec_hbm, speed_hbm, dir_hbm, coupling_hbm, out_hbm, spec, speed, dirs, coupling, amp, out, in_sems, out_sems):
    f32 = jnp.float32
    small = [
        pltpu.make_async_copy(source, target, in_sems.at[PARTS + at])
        for at, (source, target) in enumerate(((speed_hbm, speed), (dir_hbm, dirs), (coupling_hbm, coupling)))
    ]
    loads = [
        pltpu.make_async_copy(spec_hbm.at[part, :], spec.at[part, :], in_sems.at[at])
        for at, part in enumerate(pl.ds(at * PART, PART) for at in range(PARTS))
    ]
    for copy in small + loads:
        copy.start()
    for copy in small:
        copy.wait()

    row = lax.broadcasted_iota(jnp.int32, (PAIR, NFREQ), 0)
    col = lax.broadcasted_iota(jnp.int32, (PAIR, NFREQ), 1)
    spread = jnp.where(jnp.where(row >= NFREQ, row - NFREQ, row) == col, 1.0, 0.0).astype(f32)
    dims = (((1,), (1,)), ((), ()))
    best = lax.Precision.HIGHEST
    tall = lax.dot_general(spread, coupling[...], dims, precision=best, preferred_element_type=f32)
    both = lax.dot_general(tall, spread, dims, precision=best, preferred_element_type=f32)
    at = lax.broadcasted_iota(jnp.int32, (PAIR, PAIR), 0) >= NFREQ
    to = lax.broadcasted_iota(jnp.int32, (PAIR, PAIR), 1) >= NFREQ
    matrix = jnp.where(at == to, 0.2 * both, 0.0)

    angles = lax.broadcasted_iota(jnp.int32, (40, P_DEV), 0).astype(f32) * (2.0 * jnp.pi / NDIR)
    align = jnp.maximum(jnp.cos(angles - dirs[...]), 0.0)
    growth = speed[...] * align

    place = lax.broadcasted_iota(jnp.int32, (PAIR, P_DEV), 0)
    first = place < NFREQ
    phase = (jnp.where(first, place, place - NFREQ).astype(f32) + 1.0) * (1.0 / NFREQ)

    lane = lax.broadcasted_iota(jnp.int32, (8, LANES), 1)
    unused = QDEV - REST * WINDOWS
    for quad in range(4):
        begin = (QDEV * (quad + 1) - unused) * CHUNK + CHUNK - 1
        out[pl.ds(begin, unused, stride=CHUNK), :] = jnp.zeros((unused, LANES), f32)

    total = jnp.zeros((8, P_DEV), f32)
    for at, copy in enumerate(loads):
        copy.wait()
        for tile in range(PART // 8):
            begin = at * PART + tile * 8
            total = total + spec[begin : begin + 8, :]
    energy = jnp.sum(total, axis=0, keepdims=True) * (1.0 / BINS)
    amp[...] = growth - 0.5 * jnp.sqrt(energy / (energy + 1.0))

    stores = []
    for pair in range(NDIR // 2):
        low = amp[2 * pair : 2 * pair + 1, :]
        high = amp[2 * pair + 1 : 2 * pair + 2, :]
        relaxed = spec[PAIR * pair : PAIR * pair + PAIR, :] * jnp.exp(phase * jnp.where(first, low, high))
        forced = relaxed + lax.dot_general(
            matrix, relaxed, (((1,), (0,)), ((), ())), precision=lax.Precision.HIGH, preferred_element_type=f32
        )
        for tile in range(PAIR // 8):
            begin = PAIR * pair + tile * 8
            halves = [forced[tile * 8 : tile * 8 + 8, half * LANES : (half + 1) * LANES] for half in range(HALVES)]
            if begin % (2 * QUAD) == QUAD - REST:
                turned = [pltpu.roll(half, LANES // 2, 1) for half in halves]
                windows = (halves[0], jnp.where(lane < LANES // 2, turned[0], turned[1]), halves[1])
                for at in range(2):
                    for window in range(WINDOWS):
                        first_row = ((begin // QUAD + at) * QDEV + window) * CHUNK + CHUNK - 1
                        rows = pl.ds(first_row, REST, stride=WINDOWS * CHUNK)
                        out[rows, :] = windows[window][at * REST : (at + 1) * REST]
            else:
                quad = begin // QUAD
                slot, member = divmod(begin - first_bin(quad), QDEV)
                for half in range(HALVES):
                    first_row = (quad * QDEV + member) * CHUNK + HALVES * slot + half
                    out[pl.ds(first_row, 8, stride=CHUNK), :] = halves[half]
        if (2 * pair + 2) // 9 > len(stores):
            rows = pl.ds(len(stores) * QDEV * CHUNK, QDEV * CHUNK)
            stores.append(pltpu.make_async_copy(out.at[rows, :], out_hbm.at[rows, :], out_sems.at[len(stores)]))
            stores[-1].start()
    for copy in stores:
        copy.wait()


def source_terms(spectrum, wind_speed, wind_dir, coupling):
    f32 = jnp.float32
    return pl.pallas_call(
        source_kernel,
        out_shape=jax.ShapeDtypeStruct((ROWS, LANES), f32),
        in_specs=[pl.BlockSpec(memory_space=pltpu.HBM)] * 4,
        out_specs=pl.BlockSpec(memory_space=pltpu.HBM),
        scratch_shapes=[
            pltpu.VMEM((BINS, P_DEV), f32),
            pltpu.VMEM((1, P_DEV), f32),
            pltpu.VMEM((1, P_DEV), f32),
            pltpu.VMEM((NFREQ, NFREQ), f32),
            pltpu.VMEM((40, P_DEV), f32),
            pltpu.VMEM((ROWS, LANES), f32),
            pltpu.SemaphoreType.DMA((PARTS + 3,)),
            pltpu.SemaphoreType.DMA((4,)),
        ],
        compiler_params=pltpu.CompilerParams(vmem_limit_bytes=63 * 1024 * 1024),
        name="source_terms",
    )(spectrum.T, wind_speed.reshape(1, P_DEV), wind_dir.reshape(1, P_DEV), coupling)


def propagate_kernel(
    line_ref, off_ref, end_ref, up_ref, scale_ref, recv_ref, index_ref, mask_ref, spot_ref, coef_ref, out_ref, *scratch
):
    src, dst, src_rest, dst_rest, *bufs = scratch
    up_y = up_ref[0]
    lane = lax.broadcasted_iota(jnp.int32, (GROUP, LANES), 1)
    low = lax.broadcasted_iota(jnp.int32, (GROUP, LANES), 0) < HALF
    edge = lane == jnp.where(up_y > 0, 0, LANES - 1)
    shift = jnp.where(up_y > 0, 1, LANES - 1)

    pieces = [(HALVES * slot + half, slot, half * LANES * GROUP) for slot in range(SLOTS) for half in range(HALVES)]
    pieces.append((CHUNK - 1, SLOTS, up_ref[1] * (LANES // 2 * GROUP)))
    for row, slot, begin in pieces:
        part = recv_ref[pl.ds(row, N_DEV, stride=CHUNK), :].T * scale_ref[slot]
        if slot < GROUP:
            src[pl.ds(begin + slot, LANES, stride=GROUP), :] = part
        else:
            src_rest[pl.ds(begin + slot - GROUP, LANES, stride=GROUP), :] = part
            src_rest[pl.ds(begin + slot - GROUP + HALF, LANES, stride=GROUP), :] = part

    for buf in bufs:
        buf[...] = jnp.zeros_like(buf)
    bufs_rest = [bufs[2 * s : 2 * s + 2] for s in range(SUB + 1, 2 * SUB + 2)]
    bufs = [bufs[2 * s : 2 * s + 2] for s in range(SUB + 1)]
    coef_x, coef_y, rest_x, rest_y = [coef_ref[k * GROUP : (k + 1) * GROUP, :] for k in range(4)]

    def wide(ref, cell):
        return jnp.broadcast_to(ref[pl.ds(cell, 1), :], (GROUP, LANES))

    def two(ref, cell):
        return jnp.where(low, wide(ref, cell), wide(ref, cell + 2))

    def take(values, spots):
        return lax.gather(
            values, spots[:, :, None], ALONG_LANES, slice_sizes=(1, 1), mode=lax.GatherScatterMode.PROMISE_IN_BOUNDS
        )

    def lines(begin):
        return pl.ds(pl.multiple_of(begin, GROUP), GROUP)

    def at(i, j, blocks=COLS):
        begin = (i * blocks + j) * GROUP
        return slice(begin, begin + GROUP)

    def store(target, cell, taken):
        begin = line_ref[cell]
        off = off_ref[cell]
        end = end_ref[cell]
        pltpu.store(target.at[lines(begin), :], taken, mask=(lane >= off) & (lane < end))
        pltpu.store(target.at[lines(begin + GROUP), :], taken, mask=lane < end - LANES)

    def scatter(cell, values):
        store(dst, cell, take(values, wide(spot_ref, cell)))

    def scatter_rest(cell, values):
        taken = take(values, two(spot_ref, cell))
        store(dst_rest, cell, taken)
        store(dst_rest, cell + 2, pltpu.roll(taken, HALF, 0))

    def gather(cell):
        begin = line_ref[cell]
        both = jnp.where(lane >= off_ref[cell], src[lines(begin), :], src[lines(begin + GROUP), :])
        return jnp.where(wide(mask_ref, cell) > 0, take(both, wide(index_ref, cell)), 0.0)

    def gather_rest(cell):
        begin, other = line_ref[cell], line_ref[cell + 2]
        one = jnp.where(low, src_rest[lines(begin), :], src_rest[lines(other), :])
        next_one = jnp.where(low, src_rest[lines(begin + GROUP), :], src_rest[lines(other + GROUP), :])
        both = jnp.where(lane >= jnp.where(low, off_ref[cell], off_ref[cell + 2]), one, next_one)
        return jnp.where(two(mask_ref, cell) > 0, take(both, two(index_ref, cell)), 0.0)

    def turn(fields):
        return [pltpu.roll(field, shift, 1) for field in fields]

    def round_of(u, p):
        def has(delay):
            return not isinstance(u, int) or 0 <= u - delay < SLABS

        def cell_of(delay, i, j):
            return pl.multiple_of((u - delay) * STEP, STEP) + (i * COLS + j)

        steps = [step for step in range(SUB, 0, -1) if has(step)]
        above = {step: [bufs[step - 1][p][at(SLAB - 1, j), :] for j in range(COLS)] for step in steps}
        above_rest = {step: [bufs_rest[step - 1][p][at(SLAB - 1, j, 2), :] for j in range(2)] for step in steps}
        for i in range(SLAB):
            if has(SUB + 1):
                for j in range(COLS):
                    scatter(cell_of(SUB + 1, i, j), bufs[SUB][1 - p][at(i, j), :])
                for j in range(2):
                    scatter_rest(cell_of(SUB + 1, i, j), bufs_rest[SUB][1 - p][at(i, j, 2), :])
            for step in steps:
                fields = [bufs[step - 1][1 - p][at(i, j), :] for j in range(COLS)]
                turned = turn(fields)
                for j in range(COLS):
                    upwind_y = jnp.where(edge, turned[j - 1] if j else 0.0, turned[j])
                    moved = fields[j] + (coef_x * above[step][j] + coef_y * upwind_y)
                    bufs[step][p][at(i, j), :] = wide(mask_ref, cell_of(step, i, j)) * moved
                above[step] = fields
                fields = [bufs_rest[step - 1][1 - p][at(i, j, 2), :] for j in range(2)]
                turned = turn(fields)
                before = jnp.where(low, 0.0, pltpu.roll(turned[1], HALF, 0))
                for j in range(2):
                    upwind_y = jnp.where(edge, turned[0] if j else before, turned[j])
                    moved = fields[j] + (rest_x * above_rest[step][j] + rest_y * upwind_y)
                    bufs_rest[step][p][at(i, j, 2), :] = two(mask_ref, cell_of(step, i, j)) * moved
                above_rest[step] = fields
            if has(0):
                for j in range(COLS):
                    bufs[0][p][at(i, j), :] = gather(cell_of(0, i, j))
                for j in range(2):
                    bufs_rest[0][p][at(i, j, 2), :] = gather_rest(cell_of(0, i, j))

    def rounds(u, carry):
        for k in range(UNROLL):
            round_of(SUB + 1 + u * UNROLL + k, (SUB + 1 + k) % 2)
        return carry

    loops = (SLABS - SUB - 1) // UNROLL
    for u in range(SUB + 1):
        round_of(u, u % 2)
    lax.fori_loop(0, loops, rounds, 0)
    for u in range(SUB + 1 + loops * UNROLL, SLABS + SUB + 1):
        round_of(u, u % 2)

    for row, slot, begin in pieces:
        lines_of = dst if slot < GROUP else dst_rest
        part = lines_of[pl.ds(begin + slot % GROUP, LANES, stride=GROUP), :]
        out_ref[pl.ds(row, N_DEV, stride=CHUNK), :] = part.T


def propagation_tables(land_mask, sea_index):
    f32 = jnp.float32
    dev = lax.axis_index("dev")
    quad = dev // QDEV
    member = dev % QDEV
    slots = jnp.arange(HELD)
    odd = quad % 2
    whole = quad * QUAD + REST * odd + QDEV * slots + member
    left = quad * QUAD + (QUAD - REST) * (1 - odd) + member // WINDOWS
    bins = jnp.where(slots < SLOTS, whole, left)
    real = (slots < SLOTS) | ((slots == SLOTS) & (member < REST * WINDOWS))
    speeds = jnp.where(real, 0.45 * 1.1 ** (-(bins % NFREQ).astype(f32)), 0.0)
    angle = (bins // NFREQ).astype(f32) * (2.0 * jnp.pi / NDIR)
    abs_x = jnp.abs(speeds * jnp.cos(angle))
    abs_y = jnp.abs(speeds * jnp.sin(angle))
    stay = 1.0 - abs_x - abs_y
    coef_x, coef_y = abs_x / stay, abs_y / stay
    rest = [part for coef in (coef_x, coef_y) for part in 2 * [coef[GROUP : GROUP + HALF]]]
    coef = jnp.concatenate([coef_x[:GROUP], coef_y[:GROUP], *rest])
    coef = jnp.broadcast_to(coef[:, None], (4 * GROUP, LANES))
    scale = stay * stay * stay * stay
    up_x = (quad == 0) | (quad == 3)
    up_y = quad < 2

    def ordered(table):
        table = table.reshape((NXG, COLS) + table.shape[1:])
        table = jnp.where(up_x, table, jnp.flip(table, 0))
        table = jnp.where(up_y, table, jnp.flip(table, 1))
        return table.reshape((BLOCKS,) + table.shape[2:])

    mask = land_mask.reshape(BLOCKS, LANES).astype(f32)
    upto = jnp.dot(mask, jnp.triu(jnp.ones((LANES, LANES), f32)), preferred_element_type=f32)
    before = jnp.dot(jnp.tril(jnp.ones((BLOCKS, BLOCKS), f32), -1), upto[:, LANES - 1 :], preferred_element_type=f32)
    index = (before + upto - mask).astype(jnp.int32) & (LANES - 1)
    start = before[:, 0].astype(jnp.int32)
    line = start >> 7
    off = start & (LANES - 1)
    end = off + upto[:, LANES - 1].astype(jnp.int32)

    spot = (sea_index & (LANES - 1)).reshape(N_DEV, P_DEV).T.astype(f32)
    lines = jnp.arange(P_DEV)
    one = jnp.dot((line[:, None] == lines).astype(f32), spot, preferred_element_type=f32)
    two = jnp.dot((line[:, None] + 1 == lines).astype(f32), spot, preferred_element_type=f32)
    spots = jnp.where(jnp.arange(LANES) >= off[:, None], one, two).astype(jnp.int32)

    scalars = [ordered(line * GROUP), ordered(off), ordered(end), jnp.stack([up_y.astype(jnp.int32), member % WINDOWS]), scale]
    return scalars, [ordered(index), ordered(mask), ordered(spots), coef]


def propagate(recv, scalars, vectors):
    f32 = jnp.float32
    return pl.pallas_call(
        propagate_kernel,
        out_shape=jax.ShapeDtypeStruct((ROWS, LANES), f32),
        in_specs=[pl.BlockSpec(memory_space=pltpu.SMEM)] * 5 + [pl.BlockSpec(memory_space=pltpu.VMEM)] * 5,
        out_specs=pl.BlockSpec(memory_space=pltpu.VMEM),
        scratch_shapes=[pltpu.VMEM(((P_DEV + 2) * GROUP, LANES), f32)] * 4
        + [pltpu.VMEM((SLAB * COLS * GROUP, LANES), f32)] * (2 * (SUB + 1))
        + [pltpu.VMEM((SLAB * 2 * GROUP, LANES), f32)] * (2 * (SUB + 1)),
        compiler_params=pltpu.CompilerParams(vmem_limit_bytes=VMEM),
        name="propagate",
    )(*scalars, recv, *vectors)


def collect_kernel(in_ref, out_ref):
    lane = lax.broadcasted_iota(jnp.int32, (REST, LANES), 1)
    for quad in range(4):
        for half in range(HALVES):
            columns = slice(half * LANES, (half + 1) * LANES)
            for slot in range(SLOTS):
                part = in_ref[pl.ds(quad * QDEV * CHUNK + HALVES * slot + half, QDEV, stride=CHUNK), :]
                begin = first_bin(quad) + QDEV * slot
                out_ref[begin : begin + QDEV, columns] = part
        begin = QUAD * quad + (0 if quad % 2 else QUAD - REST)
        low, middle, high = [
            in_ref[pl.ds((quad * QDEV + window) * CHUNK + CHUNK - 1, REST, stride=WINDOWS * CHUNK), :]
            for window in range(WINDOWS)
        ]
        middle = pltpu.roll(middle, LANES // 2, 1)
        out_ref[begin : begin + REST, :LANES] = jnp.where(lane < OWNED[1], low, middle)
        out_ref[begin : begin + REST, LANES:] = jnp.where(lane < OWNED[2] - LANES, middle, high)


def collect(back):
    return pl.pallas_call(
        collect_kernel,
        out_shape=jax.ShapeDtypeStruct((BINS, P_DEV), jnp.float32),
        in_specs=[pl.BlockSpec(memory_space=pltpu.VMEM)],
        out_specs=pl.BlockSpec(memory_space=pltpu.VMEM),
        compiler_params=pltpu.CompilerParams(vmem_limit_bytes=VMEM),
        name="collect",
    )(back)


def exchange(rows):
    swapped = lax.all_to_all(rows.reshape(ROWS, 1, LANES), "dev", split_axis=0, concat_axis=0, tiled=True)
    return swapped.reshape(ROWS, LANES)


def on_device(spectrum, wind_speed, wind_dir, coupling, land_mask, sea_index):
    sent = source_terms(spectrum, wind_speed, wind_dir, coupling)
    moved = propagate(exchange(sent), *propagation_tables(land_mask, sea_index))
    return collect(exchange(moved)).T


def solution(mesh):
    in_specs = (P("dev", None), P("dev"), P("dev"), P(), P(), P())
    return jax.shard_map(on_device, mesh=mesh, in_specs=in_specs, out_specs=P("dev", None), check_vma=False)
```

```python
import jax
import jax.numpy as jnp
from jax import lax
from jax.experimental import pallas as pl
from jax.experimental.pallas import tpu as pltpu
from jax.sharding import PartitionSpec as P

NDIR = 36
NFREQ = 36
BINS = NDIR * NFREQ
SUB = 4
NXG = 96
NYG = 512
N_DEV = 128
P_DEV = 256
LANES = 128
COLS = NYG // LANES
BLOCKS = NXG * COLS
QUAD = BINS // 4
QDEV = N_DEV // 4
SLOTS = QUAD // QDEV
REST = QUAD - SLOTS * QDEV
WINDOWS = 3
OWNED = (0, 100, 160, 256)
GROUP = 8
HALF = GROUP // 2
HELD = 2 * GROUP
HALVES = P_DEV // LANES
CHUNK = SLOTS * HALVES + 1
ROWS = N_DEV * CHUNK
PAIR = 2 * NFREQ
PARTS = 6
PART = BINS // PARTS
SLAB = 4
SLABS = NXG // SLAB
STEP = SLAB * COLS
UNROLL = 18
ALONG_LANES = lax.GatherDimensionNumbers(
    offset_dims=(),
    collapsed_slice_dims=(1,),
    start_index_map=(1,),
    operand_batching_dims=(0,),
    start_indices_batching_dims=(0,),
)
VMEM = 48 * 1024 * 1024


def first_bin(quad):
    return QUAD * quad + REST * (quad % 2)


def source_kernel(spec_hbm, speed_hbm, dir_hbm, coupling_hbm, out_hbm, spec, speed, dirs, coupling, amp, out, in_sems, out_sems):
    f32 = jnp.float32
    small = [
        pltpu.make_async_copy(source, target, in_sems.at[PARTS + at])
        for at, (source, target) in enumerate(((speed_hbm, speed), (dir_hbm, dirs), (coupling_hbm, coupling)))
    ]
    loads = [
        pltpu.make_async_copy(spec_hbm.at[part, :], spec.at[part, :], in_sems.at[at])
        for at, part in enumerate(pl.ds(at * PART, PART) for at in range(PARTS))
    ]
    for copy in small + loads:
        copy.start()
    for copy in small:
        copy.wait()

    row = lax.broadcasted_iota(jnp.int32, (PAIR, NFREQ), 0)
    col = lax.broadcasted_iota(jnp.int32, (PAIR, NFREQ), 1)
    spread = jnp.where(jnp.where(row >= NFREQ, row - NFREQ, row) == col, 1.0, 0.0).astype(f32)
    dims = (((1,), (1,)), ((), ()))
    best = lax.Precision.HIGHEST
    tall = lax.dot_general(spread, coupling[...], dims, precision=best, preferred_element_type=f32)
    both = lax.dot_general(tall, spread, dims, precision=best, preferred_element_type=f32)
    at = lax.broadcasted_iota(jnp.int32, (PAIR, PAIR), 0) >= NFREQ
    to = lax.broadcasted_iota(jnp.int32, (PAIR, PAIR), 1) >= NFREQ
    matrix = jnp.where(at == to, 0.2 * both, 0.0)

    angles = lax.broadcasted_iota(jnp.int32, (40, P_DEV), 0).astype(f32) * (2.0 * jnp.pi / NDIR)
    align = jnp.maximum(jnp.cos(angles - dirs[...]), 0.0)
    growth = speed[...] * align

    place = lax.broadcasted_iota(jnp.int32, (PAIR, P_DEV), 0)
    first = place < NFREQ
    phase = (jnp.where(first, place, place - NFREQ).astype(f32) + 1.0) * (1.0 / NFREQ)

    lane = lax.broadcasted_iota(jnp.int32, (8, LANES), 1)
    unused = QDEV - REST * WINDOWS
    for quad in range(4):
        begin = (QDEV * (quad + 1) - unused) * CHUNK + CHUNK - 1
        out[pl.ds(begin, unused, stride=CHUNK), :] = jnp.zeros((unused, LANES), f32)

    total = jnp.zeros((8, P_DEV), f32)
    for at, copy in enumerate(loads):
        copy.wait()
        for tile in range(PART // 8):
            begin = at * PART + tile * 8
            total = total + spec[begin : begin + 8, :]
    energy = jnp.sum(total, axis=0, keepdims=True) * (1.0 / BINS)
    amp[...] = growth - 0.5 * jnp.sqrt(energy / (energy + 1.0))

    stores = []
    for pair in range(NDIR // 2):
        low = amp[2 * pair : 2 * pair + 1, :]
        high = amp[2 * pair + 1 : 2 * pair + 2, :]
        relaxed = spec[PAIR * pair : PAIR * pair + PAIR, :] * jnp.exp(phase * jnp.where(first, low, high))
        forced = relaxed + lax.dot_general(
            matrix, relaxed, (((1,), (0,)), ((), ())), precision=lax.Precision.HIGH, preferred_element_type=f32
        )
        for tile in range(PAIR // 8):
            begin = PAIR * pair + tile * 8
            halves = [forced[tile * 8 : tile * 8 + 8, half * LANES : (half + 1) * LANES] for half in range(HALVES)]
            if begin % (2 * QUAD) == QUAD - REST:
                turned = [pltpu.roll(half, LANES // 2, 1) for half in halves]
                windows = (halves[0], jnp.where(lane < LANES // 2, turned[0], turned[1]), halves[1])
                for at in range(2):
                    for window in range(WINDOWS):
                        first_row = ((begin // QUAD + at) * QDEV + window) * CHUNK + CHUNK - 1
                        rows = pl.ds(first_row, REST, stride=WINDOWS * CHUNK)
                        out[rows, :] = windows[window][at * REST : (at + 1) * REST]
            else:
                quad = begin // QUAD
                slot, member = divmod(begin - first_bin(quad), QDEV)
                for half in range(HALVES):
                    first_row = (quad * QDEV + member) * CHUNK + HALVES * slot + half
                    out[pl.ds(first_row, 8, stride=CHUNK), :] = halves[half]
        if (2 * pair + 2) // 9 > len(stores):
            rows = pl.ds(len(stores) * QDEV * CHUNK, QDEV * CHUNK)
            stores.append(pltpu.make_async_copy(out.at[rows, :], out_hbm.at[rows, :], out_sems.at[len(stores)]))
            stores[-1].start()
    for copy in stores:
        copy.wait()


def source_terms(spectrum, wind_speed, wind_dir, coupling):
    f32 = jnp.float32
    return pl.pallas_call(
        source_kernel,
        out_shape=jax.ShapeDtypeStruct((ROWS, LANES), f32),
        in_specs=[pl.BlockSpec(memory_space=pltpu.HBM)] * 4,
        out_specs=pl.BlockSpec(memory_space=pltpu.HBM),
        scratch_shapes=[
            pltpu.VMEM((BINS, P_DEV), f32),
            pltpu.VMEM((1, P_DEV), f32),
            pltpu.VMEM((1, P_DEV), f32),
            pltpu.VMEM((NFREQ, NFREQ), f32),
            pltpu.VMEM((40, P_DEV), f32),
            pltpu.VMEM((ROWS, LANES), f32),
            pltpu.SemaphoreType.DMA((PARTS + 3,)),
            pltpu.SemaphoreType.DMA((4,)),
        ],
        compiler_params=pltpu.CompilerParams(vmem_limit_bytes=63 * 1024 * 1024),
        name="source_terms",
    )(spectrum.T, wind_speed.reshape(1, P_DEV), wind_dir.reshape(1, P_DEV), coupling)


def propagate_kernel(
    line_ref, off_ref, up_ref, scale_ref, recv_ref, index_ref, mask_ref, spot_ref, turn_ref, coef_ref, out_ref, *scratch
):
    src, dst, src_rest, dst_rest, *bufs = scratch
    up_y = up_ref[0]
    lane = lax.broadcasted_iota(jnp.int32, (GROUP, LANES), 1)
    low = lax.broadcasted_iota(jnp.int32, (GROUP, LANES), 0) < HALF
    edge = lane == jnp.where(up_y > 0, 0, LANES - 1)
    shift = jnp.where(up_y > 0, 1, LANES - 1)

    pieces = [(HALVES * slot + half, slot, half * LANES * GROUP) for slot in range(SLOTS) for half in range(HALVES)]
    pieces.append((CHUNK - 1, SLOTS, up_ref[1] * (LANES // 2 * GROUP)))
    for row, slot, begin in pieces:
        part = recv_ref[pl.ds(row, N_DEV, stride=CHUNK), :].T * scale_ref[slot]
        if slot < GROUP:
            src[pl.ds(begin + slot, LANES, stride=GROUP), :] = part
        else:
            src_rest[pl.ds(begin + slot - GROUP, LANES, stride=GROUP), :] = part
            src_rest[pl.ds(begin + slot - GROUP + HALF, LANES, stride=GROUP), :] = part

    for buf in bufs:
        buf[...] = jnp.zeros_like(buf)
    bufs_rest = [bufs[2 * s : 2 * s + 2] for s in range(SUB + 1, 2 * SUB + 2)]
    bufs = [bufs[2 * s : 2 * s + 2] for s in range(SUB + 1)]
    coef_x, coef_y, rest_x, rest_y = [coef_ref[k * GROUP : (k + 1) * GROUP, :] for k in range(4)]

    def wide(ref, cell):
        return jnp.broadcast_to(ref[pl.ds(cell, 1), :], (GROUP, LANES))

    def two(ref, cell):
        return jnp.where(low, wide(ref, cell), wide(ref, cell + 2))

    def take(values, spots):
        return lax.gather(
            values, spots[:, :, None], ALONG_LANES, slice_sizes=(1, 1), mode=lax.GatherScatterMode.PROMISE_IN_BOUNDS
        )

    def lines(begin):
        return pl.ds(pl.multiple_of(begin, GROUP), GROUP)

    def at(i, j, blocks=COLS):
        begin = (i * blocks + j) * GROUP
        return slice(begin, begin + GROUP)

    def store(target, cell, taken):
        begin = line_ref[cell]
        turn_of = wide(turn_ref, cell)
        pltpu.store(target.at[lines(begin), :], taken, mask=turn_of == 1)
        pltpu.store(target.at[lines(begin + GROUP), :], taken, mask=turn_of == 2)

    def scatter(cell, values):
        store(dst, cell, take(values, wide(spot_ref, cell)))

    def scatter_rest(cell, values):
        taken = take(values, two(spot_ref, cell))
        store(dst_rest, cell, taken)
        store(dst_rest, cell + 2, pltpu.roll(taken, HALF, 0))

    def gather(cell):
        begin = line_ref[cell]
        both = jnp.where(lane >= off_ref[cell], src[lines(begin), :], src[lines(begin + GROUP), :])
        return jnp.where(wide(mask_ref, cell) > 0, take(both, wide(index_ref, cell)), 0.0)

    def gather_rest(cell):
        begin, other = line_ref[cell], line_ref[cell + 2]
        one = jnp.where(low, src_rest[lines(begin), :], src_rest[lines(other), :])
        next_one = jnp.where(low, src_rest[lines(begin + GROUP), :], src_rest[lines(other + GROUP), :])
        both = jnp.where(lane >= jnp.where(low, off_ref[cell], off_ref[cell + 2]), one, next_one)
        return jnp.where(two(mask_ref, cell) > 0, take(both, two(index_ref, cell)), 0.0)

    def turn(fields):
        return [pltpu.roll(field, shift, 1) for field in fields]

    def round_of(u, p):
        def has(delay):
            return not isinstance(u, int) or 0 <= u - delay < SLABS

        def cell_of(delay, i, j):
            return pl.multiple_of((u - delay) * STEP, STEP) + (i * COLS + j)

        steps = [step for step in range(SUB, 0, -1) if has(step)]
        above = {step: [bufs[step - 1][p][at(SLAB - 1, j), :] for j in range(COLS)] for step in steps}
        above_rest = {step: [bufs_rest[step - 1][p][at(SLAB - 1, j, 2), :] for j in range(2)] for step in steps}
        for i in range(SLAB):
            if has(SUB + 1):
                for j in range(COLS):
                    scatter(cell_of(SUB + 1, i, j), bufs[SUB][1 - p][at(i, j), :])
                for j in range(2):
                    scatter_rest(cell_of(SUB + 1, i, j), bufs_rest[SUB][1 - p][at(i, j, 2), :])
            for step in steps:
                fields = [bufs[step - 1][1 - p][at(i, j), :] for j in range(COLS)]
                turned = turn(fields)
                for j in range(COLS):
                    upwind_y = jnp.where(edge, turned[j - 1] if j else 0.0, turned[j])
                    moved = fields[j] + (coef_x * above[step][j] + coef_y * upwind_y)
                    bufs[step][p][at(i, j), :] = wide(mask_ref, cell_of(step, i, j)) * moved
                above[step] = fields
                fields = [bufs_rest[step - 1][1 - p][at(i, j, 2), :] for j in range(2)]
                turned = turn(fields)
                before = jnp.where(low, 0.0, pltpu.roll(turned[1], HALF, 0))
                for j in range(2):
                    upwind_y = jnp.where(edge, turned[0] if j else before, turned[j])
                    moved = fields[j] + (rest_x * above_rest[step][j] + rest_y * upwind_y)
                    bufs_rest[step][p][at(i, j, 2), :] = two(mask_ref, cell_of(step, i, j)) * moved
                above_rest[step] = fields
            if has(0):
                for j in range(COLS):
                    bufs[0][p][at(i, j), :] = gather(cell_of(0, i, j))
                for j in range(2):
                    bufs_rest[0][p][at(i, j, 2), :] = gather_rest(cell_of(0, i, j))

    def rounds(u, carry):
        for k in range(UNROLL):
            round_of(SUB + 1 + u * UNROLL + k, (SUB + 1 + k) % 2)
        return carry

    loops = (SLABS - SUB - 1) // UNROLL
    for u in range(SUB + 1):
        round_of(u, u % 2)
    lax.fori_loop(0, loops, rounds, 0)
    for u in range(SUB + 1 + loops * UNROLL, SLABS + SUB + 1):
        round_of(u, u % 2)

    for row, slot, begin in pieces:
        lines_of = dst if slot < GROUP else dst_rest
        part = lines_of[pl.ds(begin + slot % GROUP, LANES, stride=GROUP), :]
        out_ref[pl.ds(row, N_DEV, stride=CHUNK), :] = part.T


def propagation_tables(land_mask, sea_index):
    f32 = jnp.float32
    dev = lax.axis_index("dev")
    quad = dev // QDEV
    member = dev % QDEV
    slots = jnp.arange(HELD)
    odd = quad % 2
    whole = quad * QUAD + REST * odd + QDEV * slots + member
    left = quad * QUAD + (QUAD - REST) * (1 - odd) + member // WINDOWS
    bins = jnp.where(slots < SLOTS, whole, left)
    real = (slots < SLOTS) | ((slots == SLOTS) & (member < REST * WINDOWS))
    speeds = jnp.where(real, 0.45 * 1.1 ** (-(bins % NFREQ).astype(f32)), 0.0)
    angle = (bins // NFREQ).astype(f32) * (2.0 * jnp.pi / NDIR)
    abs_x = jnp.abs(speeds * jnp.cos(angle))
    abs_y = jnp.abs(speeds * jnp.sin(angle))
    stay = 1.0 - abs_x - abs_y
    coef_x, coef_y = abs_x / stay, abs_y / stay
    rest = [part for coef in (coef_x, coef_y) for part in 2 * [coef[GROUP : GROUP + HALF]]]
    coef = jnp.concatenate([coef_x[:GROUP], coef_y[:GROUP], *rest])
    coef = jnp.broadcast_to(coef[:, None], (4 * GROUP, LANES))
    scale = stay * stay * stay * stay
    up_x = (quad == 0) | (quad == 3)
    up_y = quad < 2

    def ordered(table):
        table = table.reshape((NXG, COLS) + table.shape[1:])
        table = jnp.where(up_x, table, jnp.flip(table, 0))
        table = jnp.where(up_y, table, jnp.flip(table, 1))
        return table.reshape((BLOCKS,) + table.shape[2:])

    mask = land_mask.reshape(BLOCKS, LANES).astype(f32)
    upto = jnp.dot(mask, jnp.triu(jnp.ones((LANES, LANES), f32)), preferred_element_type=f32)
    before = jnp.dot(jnp.tril(jnp.ones((BLOCKS, BLOCKS), f32), -1), upto[:, LANES - 1 :], preferred_element_type=f32)
    index = (before + upto - mask).astype(jnp.int32) & (LANES - 1)
    start = before[:, 0].astype(jnp.int32)
    line = start >> 7
    off = start & (LANES - 1)
    end = off + upto[:, LANES - 1].astype(jnp.int32)

    spot = (sea_index & (LANES - 1)).reshape(N_DEV, P_DEV).T.astype(f32)
    lines = jnp.arange(P_DEV)
    one = jnp.dot((line[:, None] == lines).astype(f32), spot, preferred_element_type=f32)
    two = jnp.dot((line[:, None] + 1 == lines).astype(f32), spot, preferred_element_type=f32)
    spots = jnp.where(jnp.arange(LANES) >= off[:, None], one, two).astype(jnp.int32)

    first = (jnp.arange(LANES) >= off[:, None]) & (jnp.arange(LANES) < end[:, None])
    turns = jnp.where(first, 1, jnp.where(jnp.arange(LANES) < end[:, None] - LANES, 2, 0)).astype(jnp.int32)

    scalars = [ordered(line * GROUP), ordered(off), jnp.stack([up_y.astype(jnp.int32), member % WINDOWS]), scale]
    return scalars, [ordered(index), ordered(mask), ordered(spots), ordered(turns), coef]


def propagate(recv, scalars, vectors):
    f32 = jnp.float32
    return pl.pallas_call(
        propagate_kernel,
        out_shape=jax.ShapeDtypeStruct((ROWS, LANES), f32),
        in_specs=[pl.BlockSpec(memory_space=pltpu.SMEM)] * 4 + [pl.BlockSpec(memory_space=pltpu.VMEM)] * 6,
        out_specs=pl.BlockSpec(memory_space=pltpu.VMEM),
        scratch_shapes=[pltpu.VMEM(((P_DEV + 2) * GROUP, LANES), f32)] * 4
        + [pltpu.VMEM((SLAB * COLS * GROUP, LANES), f32)] * (2 * (SUB + 1))
        + [pltpu.VMEM((SLAB * 2 * GROUP, LANES), f32)] * (2 * (SUB + 1)),
        compiler_params=pltpu.CompilerParams(vmem_limit_bytes=VMEM),
        name="propagate",
    )(*scalars, recv, *vectors)


def collect_kernel(in_ref, out_ref):
    lane = lax.broadcasted_iota(jnp.int32, (REST, LANES), 1)
    for quad in range(4):
        for half in range(HALVES):
            columns = slice(half * LANES, (half + 1) * LANES)
            for slot in range(SLOTS):
                part = in_ref[pl.ds(quad * QDEV * CHUNK + HALVES * slot + half, QDEV, stride=CHUNK), :]
                begin = first_bin(quad) + QDEV * slot
                out_ref[begin : begin + QDEV, columns] = part
        begin = QUAD * quad + (0 if quad % 2 else QUAD - REST)
        low, middle, high = [
            in_ref[pl.ds((quad * QDEV + window) * CHUNK + CHUNK - 1, REST, stride=WINDOWS * CHUNK), :]
            for window in range(WINDOWS)
        ]
        middle = pltpu.roll(middle, LANES // 2, 1)
        out_ref[begin : begin + REST, :LANES] = jnp.where(lane < OWNED[1], low, middle)
        out_ref[begin : begin + REST, LANES:] = jnp.where(lane < OWNED[2] - LANES, middle, high)


def collect(back):
    return pl.pallas_call(
        collect_kernel,
        out_shape=jax.ShapeDtypeStruct((BINS, P_DEV), jnp.float32),
        in_specs=[pl.BlockSpec(memory_space=pltpu.VMEM)],
        out_specs=pl.BlockSpec(memory_space=pltpu.VMEM),
        compiler_params=pltpu.CompilerParams(vmem_limit_bytes=VMEM),
        name="collect",
    )(back)


def exchange(rows):
    swapped = lax.all_to_all(rows.reshape(ROWS, 1, LANES), "dev", split_axis=0, concat_axis=0, tiled=True)
    return swapped.reshape(ROWS, LANES)


def on_device(spectrum, wind_speed, wind_dir, coupling, land_mask, sea_index):
    sent = source_terms(spectrum, wind_speed, wind_dir, coupling)
    moved = propagate(exchange(sent), *propagation_tables(land_mask, sea_index))
    return collect(exchange(moved)).T


def solution(mesh):
    in_specs = (P("dev", None), P("dev"), P("dev"), P(), P(), P())
    return jax.shard_map(on_device, mesh=mesh, in_specs=in_specs, out_specs=P("dev", None), check_vma=False)
```

```python
import jax
import jax.numpy as jnp
from jax import lax
from jax.experimental import pallas as pl
from jax.experimental.pallas import tpu as pltpu
from jax.sharding import PartitionSpec as P

NDIR = 36
NFREQ = 36
BINS = NDIR * NFREQ
SUB = 4
NXG = 96
NYG = 512
N_DEV = 128
P_DEV = 256
LANES = 128
COLS = NYG // LANES
BLOCKS = NXG * COLS
QUAD = BINS // 4
QDEV = N_DEV // 4
SLOTS = QUAD // QDEV
REST = QUAD - SLOTS * QDEV
WINDOWS = 3
OWNED = (0, 100, 160, 256)
GROUP = 8
HALF = GROUP // 2
HELD = 2 * GROUP
HALVES = P_DEV // LANES
CHUNK = SLOTS * HALVES + 1
ROWS = N_DEV * CHUNK
PAIR = 2 * NFREQ
PARTS = 6
PART = BINS // PARTS
SLAB = 4
SLABS = NXG // SLAB
STEP = SLAB * COLS
UNROLL = 18
ALONG_LANES = lax.GatherDimensionNumbers(
    offset_dims=(),
    collapsed_slice_dims=(1,),
    start_index_map=(1,),
    operand_batching_dims=(0,),
    start_indices_batching_dims=(0,),
)
VMEM = 48 * 1024 * 1024


def first_bin(quad):
    return QUAD * quad + REST * (quad % 2)


def source_kernel(spec_hbm, speed_hbm, dir_hbm, coupling_hbm, out_hbm, spec, speed, dirs, coupling, amp, out, in_sems, out_sems):
    f32 = jnp.float32
    small = [
        pltpu.make_async_copy(source, target, in_sems.at[PARTS + at])
        for at, (source, target) in enumerate(((speed_hbm, speed), (dir_hbm, dirs), (coupling_hbm, coupling)))
    ]
    loads = [
        pltpu.make_async_copy(spec_hbm.at[part, :], spec.at[part, :], in_sems.at[at])
        for at, part in enumerate(pl.ds(at * PART, PART) for at in range(PARTS))
    ]
    for copy in small + loads:
        copy.start()
    for copy in small:
        copy.wait()

    row = lax.broadcasted_iota(jnp.int32, (PAIR, NFREQ), 0)
    col = lax.broadcasted_iota(jnp.int32, (PAIR, NFREQ), 1)
    spread = jnp.where(jnp.where(row >= NFREQ, row - NFREQ, row) == col, 1.0, 0.0).astype(f32)
    dims = (((1,), (1,)), ((), ()))
    best = lax.Precision.HIGHEST
    tall = lax.dot_general(spread, coupling[...], dims, precision=best, preferred_element_type=f32)
    both = lax.dot_general(tall, spread, dims, precision=best, preferred_element_type=f32)
    at = lax.broadcasted_iota(jnp.int32, (PAIR, PAIR), 0) >= NFREQ
    to = lax.broadcasted_iota(jnp.int32, (PAIR, PAIR), 1) >= NFREQ
    matrix = jnp.where(at == to, 0.2 * both, 0.0)

    angles = lax.broadcasted_iota(jnp.int32, (40, P_DEV), 0).astype(f32) * (2.0 * jnp.pi / NDIR)
    align = jnp.maximum(jnp.cos(angles - dirs[...]), 0.0)
    growth = speed[...] * align

    place = lax.broadcasted_iota(jnp.int32, (PAIR, P_DEV), 0)
    first = place < NFREQ
    phase = (jnp.where(first, place, place - NFREQ).astype(f32) + 1.0) * (1.0 / NFREQ)

    lane = lax.broadcasted_iota(jnp.int32, (8, LANES), 1)
    unused = QDEV - REST * WINDOWS
    for quad in range(4):
        begin = (QDEV * (quad + 1) - unused) * CHUNK + CHUNK - 1
        out[pl.ds(begin, unused, stride=CHUNK), :] = jnp.zeros((unused, LANES), f32)

    total = jnp.zeros((8, P_DEV), f32)
    for at, copy in enumerate(loads):
        copy.wait()
        for tile in range(PART // 8):
            begin = at * PART + tile * 8
            total = total + spec[begin : begin + 8, :]
    energy = jnp.sum(total, axis=0, keepdims=True) * (1.0 / BINS)
    amp[...] = growth - 0.5 * jnp.sqrt(energy / (energy + 1.0))

    stores = []
    for pair in range(NDIR // 2):
        low = amp[2 * pair : 2 * pair + 1, :]
        high = amp[2 * pair + 1 : 2 * pair + 2, :]
        relaxed = spec[PAIR * pair : PAIR * pair + PAIR, :] * jnp.exp(phase * jnp.where(first, low, high))
        forced = relaxed + lax.dot_general(
            matrix, relaxed, (((1,), (0,)), ((), ())), precision=lax.Precision.HIGH, preferred_element_type=f32
        )
        for tile in range(PAIR // 8):
            begin = PAIR * pair + tile * 8
            halves = [forced[tile * 8 : tile * 8 + 8, half * LANES : (half + 1) * LANES] for half in range(HALVES)]
            if begin % (2 * QUAD) == QUAD - REST:
                turned = [pltpu.roll(half, LANES // 2, 1) for half in halves]
                windows = (halves[0], jnp.where(lane < LANES // 2, turned[0], turned[1]), halves[1])
                for at in range(2):
                    for window in range(WINDOWS):
                        first_row = ((begin // QUAD + at) * QDEV + window) * CHUNK + CHUNK - 1
                        rows = pl.ds(first_row, REST, stride=WINDOWS * CHUNK)
                        out[rows, :] = windows[window][at * REST : (at + 1) * REST]
            else:
                quad = begin // QUAD
                slot, member = divmod(begin - first_bin(quad), QDEV)
                for half in range(HALVES):
                    first_row = (quad * QDEV + member) * CHUNK + HALVES * slot + half
                    out[pl.ds(first_row, 8, stride=CHUNK), :] = halves[half]
        if (2 * pair + 2) // 9 > len(stores):
            rows = pl.ds(len(stores) * QDEV * CHUNK, QDEV * CHUNK)
            stores.append(pltpu.make_async_copy(out.at[rows, :], out_hbm.at[rows, :], out_sems.at[len(stores)]))
            stores[-1].start()
    for copy in stores:
        copy.wait()


def source_terms(spectrum, wind_speed, wind_dir, coupling):
    f32 = jnp.float32
    return pl.pallas_call(
        source_kernel,
        out_shape=jax.ShapeDtypeStruct((ROWS, LANES), f32),
        in_specs=[pl.BlockSpec(memory_space=pltpu.HBM)] * 4,
        out_specs=pl.BlockSpec(memory_space=pltpu.HBM),
        scratch_shapes=[
            pltpu.VMEM((BINS, P_DEV), f32),
            pltpu.VMEM((1, P_DEV), f32),
            pltpu.VMEM((1, P_DEV), f32),
            pltpu.VMEM((NFREQ, NFREQ), f32),
            pltpu.VMEM((40, P_DEV), f32),
            pltpu.VMEM((ROWS, LANES), f32),
            pltpu.SemaphoreType.DMA((PARTS + 3,)),
            pltpu.SemaphoreType.DMA((4,)),
        ],
        compiler_params=pltpu.CompilerParams(vmem_limit_bytes=63 * 1024 * 1024),
        name="source_terms",
    )(spectrum.T, wind_speed.reshape(1, P_DEV), wind_dir.reshape(1, P_DEV), coupling)


def propagate_kernel(
    meta_ref, recv_ref, index_ref, mask_ref, spot_ref, turn_ref, coef_ref, out_ref, *scratch
):
    src, dst, src_rest, dst_rest, *bufs = scratch
    up_y = meta_ref[2 * BLOCKS]
    lane = lax.broadcasted_iota(jnp.int32, (GROUP, LANES), 1)
    low = lax.broadcasted_iota(jnp.int32, (GROUP, LANES), 0) < HALF
    edge = lane == jnp.where(up_y > 0, 0, LANES - 1)
    shift = jnp.where(up_y > 0, 1, LANES - 1)

    pieces = [(HALVES * slot + half, slot, half * LANES * GROUP) for slot in range(SLOTS) for half in range(HALVES)]
    pieces.append((CHUNK - 1, SLOTS, meta_ref[2 * BLOCKS + 1] * (LANES // 2 * GROUP)))
    for row, slot, begin in pieces:
        part = recv_ref[pl.ds(row, N_DEV, stride=CHUNK), :].T * coef_ref[4 * GROUP + slot : 4 * GROUP + slot + 1, :]
        if slot < GROUP:
            src[pl.ds(begin + slot, LANES, stride=GROUP), :] = part
        else:
            src_rest[pl.ds(begin + slot - GROUP, LANES, stride=GROUP), :] = part
            src_rest[pl.ds(begin + slot - GROUP + HALF, LANES, stride=GROUP), :] = part

    for buf in bufs:
        buf[...] = jnp.zeros_like(buf)
    bufs_rest = [bufs[2 * s : 2 * s + 2] for s in range(SUB + 1, 2 * SUB + 2)]
    bufs = [bufs[2 * s : 2 * s + 2] for s in range(SUB + 1)]
    coef_x, coef_y, rest_x, rest_y = [coef_ref[k * GROUP : (k + 1) * GROUP, :] for k in range(4)]

    def wide(ref, cell):
        return jnp.broadcast_to(ref[pl.ds(cell, 1), :], (GROUP, LANES))

    def two(ref, cell):
        return jnp.where(low, wide(ref, cell), wide(ref, cell + 2))

    def take(values, spots):
        return lax.gather(
            values, spots[:, :, None], ALONG_LANES, slice_sizes=(1, 1), mode=lax.GatherScatterMode.PROMISE_IN_BOUNDS
        )

    def lines(begin):
        return pl.ds(pl.multiple_of(begin, GROUP), GROUP)

    def at(i, j, blocks=COLS):
        begin = (i * blocks + j) * GROUP
        return slice(begin, begin + GROUP)

    def store(target, cell, taken):
        begin = meta_ref[cell]
        turn_of = wide(turn_ref, cell)
        pltpu.store(target.at[lines(begin), :], taken, mask=turn_of == 1)
        pltpu.store(target.at[lines(begin + GROUP), :], taken, mask=turn_of == 2)

    def scatter(cell, values):
        store(dst, cell, take(values, wide(spot_ref, cell)))

    def scatter_rest(cell, values):
        taken = take(values, two(spot_ref, cell))
        store(dst_rest, cell, taken)
        store(dst_rest, cell + 2, pltpu.roll(taken, HALF, 0))

    def gather(cell):
        begin = meta_ref[cell]
        both = jnp.where(lane >= meta_ref[BLOCKS + cell], src[lines(begin), :], src[lines(begin + GROUP), :])
        return jnp.where(wide(mask_ref, cell) > 0, take(both, wide(index_ref, cell)), 0.0)

    def gather_rest(cell):
        begin, other = meta_ref[cell], meta_ref[cell + 2]
        one = jnp.where(low, src_rest[lines(begin), :], src_rest[lines(other), :])
        next_one = jnp.where(low, src_rest[lines(begin + GROUP), :], src_rest[lines(other + GROUP), :])
        both = jnp.where(lane >= jnp.where(low, meta_ref[BLOCKS + cell], meta_ref[BLOCKS + cell + 2]), one, next_one)
        return jnp.where(two(mask_ref, cell) > 0, take(both, two(index_ref, cell)), 0.0)

    def turn(fields):
        return [pltpu.roll(field, shift, 1) for field in fields]

    def round_of(u, p):
        def has(delay):
            return not isinstance(u, int) or 0 <= u - delay < SLABS

        def cell_of(delay, i, j):
            return pl.multiple_of((u - delay) * STEP, STEP) + (i * COLS + j)

        steps = [step for step in range(SUB, 0, -1) if has(step)]
        above = {step: [bufs[step - 1][p][at(SLAB - 1, j), :] for j in range(COLS)] for step in steps}
        above_rest = {step: [bufs_rest[step - 1][p][at(SLAB - 1, j, 2), :] for j in range(2)] for step in steps}
        for i in range(SLAB):
            if has(SUB + 1):
                for j in range(COLS):
                    scatter(cell_of(SUB + 1, i, j), bufs[SUB][1 - p][at(i, j), :])
                for j in range(2):
                    scatter_rest(cell_of(SUB + 1, i, j), bufs_rest[SUB][1 - p][at(i, j, 2), :])
            for step in steps:
                fields = [bufs[step - 1][1 - p][at(i, j), :] for j in range(COLS)]
                turned = turn(fields)
                for j in range(COLS):
                    upwind_y = jnp.where(edge, turned[j - 1] if j else 0.0, turned[j])
                    moved = fields[j] + (coef_x * above[step][j] + coef_y * upwind_y)
                    bufs[step][p][at(i, j), :] = wide(mask_ref, cell_of(step, i, j)) * moved
                above[step] = fields
                fields = [bufs_rest[step - 1][1 - p][at(i, j, 2), :] for j in range(2)]
                turned = turn(fields)
                before = jnp.where(low, 0.0, pltpu.roll(turned[1], HALF, 0))
                for j in range(2):
                    upwind_y = jnp.where(edge, turned[0] if j else before, turned[j])
                    moved = fields[j] + (rest_x * above_rest[step][j] + rest_y * upwind_y)
                    bufs_rest[step][p][at(i, j, 2), :] = two(mask_ref, cell_of(step, i, j)) * moved
                above_rest[step] = fields
            if has(0):
                for j in range(COLS):
                    bufs[0][p][at(i, j), :] = gather(cell_of(0, i, j))
                for j in range(2):
                    bufs_rest[0][p][at(i, j, 2), :] = gather_rest(cell_of(0, i, j))

    def rounds(u, carry):
        for k in range(UNROLL):
            round_of(SUB + 1 + u * UNROLL + k, (SUB + 1 + k) % 2)
        return carry

    loops = (SLABS - SUB - 1) // UNROLL
    for u in range(SUB + 1):
        round_of(u, u % 2)
    lax.fori_loop(0, loops, rounds, 0)
    for u in range(SUB + 1 + loops * UNROLL, SLABS + SUB + 1):
        round_of(u, u % 2)

    for row, slot, begin in pieces:
        lines_of = dst if slot < GROUP else dst_rest
        part = lines_of[pl.ds(begin + slot % GROUP, LANES, stride=GROUP), :]
        out_ref[pl.ds(row, N_DEV, stride=CHUNK), :] = part.T


def propagation_tables(land_mask, sea_index):
    f32 = jnp.float32
    dev = lax.axis_index("dev")
    quad = dev // QDEV
    member = dev % QDEV
    slots = jnp.arange(HELD)
    odd = quad % 2
    whole = quad * QUAD + REST * odd + QDEV * slots + member
    left = quad * QUAD + (QUAD - REST) * (1 - odd) + member // WINDOWS
    bins = jnp.where(slots < SLOTS, whole, left)
    real = (slots < SLOTS) | ((slots == SLOTS) & (member < REST * WINDOWS))
    speeds = jnp.where(real, 0.45 * 1.1 ** (-(bins % NFREQ).astype(f32)), 0.0)
    angle = (bins // NFREQ).astype(f32) * (2.0 * jnp.pi / NDIR)
    abs_x = jnp.abs(speeds * jnp.cos(angle))
    abs_y = jnp.abs(speeds * jnp.sin(angle))
    stay = 1.0 - abs_x - abs_y
    scale = stay * stay * stay * stay
    coef_x, coef_y = abs_x / stay, abs_y / stay
    rest = [part for coef in (coef_x, coef_y) for part in 2 * [coef[GROUP : GROUP + HALF]]]
    coef = jnp.concatenate([coef_x[:GROUP], coef_y[:GROUP], *rest, scale])
    coef = jnp.broadcast_to(coef[:, None], (4 * GROUP + HELD, LANES))
    up_x = (quad == 0) | (quad == 3)
    up_y = quad < 2

    def ordered(table):
        table = table.reshape((NXG, COLS) + table.shape[1:])
        table = jnp.where(up_x, table, jnp.flip(table, 0))
        table = jnp.where(up_y, table, jnp.flip(table, 1))
        return table.reshape((BLOCKS,) + table.shape[2:])

    mask = land_mask.reshape(BLOCKS, LANES).astype(f32)
    upto = jnp.dot(mask, jnp.triu(jnp.ones((LANES, LANES), f32)), preferred_element_type=f32)
    before = jnp.dot(jnp.tril(jnp.ones((BLOCKS, BLOCKS), f32), -1), upto[:, LANES - 1 :], preferred_element_type=f32)
    index = (before + upto - mask).astype(jnp.int32) & (LANES - 1)
    start = before[:, 0].astype(jnp.int32)
    line = start >> 7
    off = start & (LANES - 1)
    end = off + upto[:, LANES - 1].astype(jnp.int32)

    spot = (sea_index & (LANES - 1)).reshape(N_DEV, P_DEV).T.astype(f32)
    lines = jnp.arange(P_DEV)
    one = jnp.dot((line[:, None] == lines).astype(f32), spot, preferred_element_type=f32)
    two = jnp.dot((line[:, None] + 1 == lines).astype(f32), spot, preferred_element_type=f32)
    spots = jnp.where(jnp.arange(LANES) >= off[:, None], one, two).astype(jnp.int32)

    first = (jnp.arange(LANES) >= off[:, None]) & (jnp.arange(LANES) < end[:, None])
    turns = jnp.where(first, 1, jnp.where(jnp.arange(LANES) < end[:, None] - LANES, 2, 0)).astype(jnp.int32)

    signs = jnp.stack([up_y.astype(jnp.int32), member % WINDOWS])
    meta = jnp.concatenate([ordered(line * GROUP), ordered(off), signs])
    return meta, [ordered(index), ordered(mask), ordered(spots), ordered(turns), coef]


def propagate(recv, meta, vectors):
    f32 = jnp.float32
    return pl.pallas_call(
        propagate_kernel,
        out_shape=jax.ShapeDtypeStruct((ROWS, LANES), f32),
        in_specs=[pl.BlockSpec(memory_space=pltpu.SMEM)] + [pl.BlockSpec(memory_space=pltpu.VMEM)] * 6,
        out_specs=pl.BlockSpec(memory_space=pltpu.VMEM),
        scratch_shapes=[pltpu.VMEM(((P_DEV + 2) * GROUP, LANES), f32)] * 4
        + [pltpu.VMEM((SLAB * COLS * GROUP, LANES), f32)] * (2 * (SUB + 1))
        + [pltpu.VMEM((SLAB * 2 * GROUP, LANES), f32)] * (2 * (SUB + 1)),
        compiler_params=pltpu.CompilerParams(vmem_limit_bytes=VMEM),
        name="propagate",
    )(meta, recv, *vectors)


def collect_kernel(in_ref, out_ref):
    lane = lax.broadcasted_iota(jnp.int32, (REST, LANES), 1)
    for quad in range(4):
        for half in range(HALVES):
            columns = slice(half * LANES, (half + 1) * LANES)
            for slot in range(SLOTS):
                part = in_ref[pl.ds(quad * QDEV * CHUNK + HALVES * slot + half, QDEV, stride=CHUNK), :]
                begin = first_bin(quad) + QDEV * slot
                out_ref[begin : begin + QDEV, columns] = part
        begin = QUAD * quad + (0 if quad % 2 else QUAD - REST)
        low, middle, high = [
            in_ref[pl.ds((quad * QDEV + window) * CHUNK + CHUNK - 1, REST, stride=WINDOWS * CHUNK), :]
            for window in range(WINDOWS)
        ]
        middle = pltpu.roll(middle, LANES // 2, 1)
        out_ref[begin : begin + REST, :LANES] = jnp.where(lane < OWNED[1], low, middle)
        out_ref[begin : begin + REST, LANES:] = jnp.where(lane < OWNED[2] - LANES, middle, high)


def collect(back):
    return pl.pallas_call(
        collect_kernel,
        out_shape=jax.ShapeDtypeStruct((BINS, P_DEV), jnp.float32),
        in_specs=[pl.BlockSpec(memory_space=pltpu.VMEM)],
        out_specs=pl.BlockSpec(memory_space=pltpu.VMEM),
        compiler_params=pltpu.CompilerParams(vmem_limit_bytes=VMEM),
        name="collect",
    )(back)


def exchange(rows):
    swapped = lax.all_to_all(rows.reshape(ROWS, 1, LANES), "dev", split_axis=0, concat_axis=0, tiled=True)
    return swapped.reshape(ROWS, LANES)


def on_device(spectrum, wind_speed, wind_dir, coupling, land_mask, sea_index):
    sent = source_terms(spectrum, wind_speed, wind_dir, coupling)
    moved = propagate(exchange(sent), *propagation_tables(land_mask, sea_index))
    return collect(exchange(moved)).T


def solution(mesh):
    in_specs = (P("dev", None), P("dev"), P("dev"), P(), P(), P())
    return jax.shard_map(on_device, mesh=mesh, in_specs=in_specs, out_specs=P("dev", None), check_vma=False)
```
